256 devices in a mesh: dp: 8 (over z_lo, y), frame: 8 (over x, core), row: 4 (over z_hi).
Axes of the slice: x: 4, y: 4, z: 8 (z_hi: 4, z_lo: 2; z = z_hi * 2 + z_lo), core: 2. Of those that a mesh axis runs over, the one named last changes fastest.
Arguments:
- latents: bfloat16 [8, 8, 32, 32, 640], P('dp', 'frame', 'row'), may hold values from -6 to 6
- space_kernel: bfloat16 [3, 3, 640, 640], replicated, may hold values from -0.078125 to 0.078125
- time_kernel: bfloat16 [1920, 640], P('dp'), may hold values from -0.125 to 0.125
- qkv_weight: bfloat16 [640, 1920], P('dp'), may hold values from -4 to 4
- out_weight: bfloat16 [640, 640], P('dp'), may hold values from -0.25 to 0.25
- norm_gain: float32 [640], replicated, may hold values from 0.25 to 1.75
- grad_out: bfloat16 [8, 8, 32, 32, 640], P('dp', 'frame', 'row'), may hold values from -6 to 6
Outputs:
- grad_latents: bfloat16 [8, 8, 32, 32, 640], P('dp', 'frame', 'row')
- grad_qkv: float32 [640, 1920], P('dp', ('frame', 'row'))
- grad_outproj: float32 [640, 640], P('dp', ('frame', 'row'))
The draws below stay inside these ranges and needn't reach their ends.
All inputs are finite; a program needn't handle non-finite values.
Results may differ from the reference program's by a relative error of at most 0.04.
Values may be sent and summed in bfloat16 or wider, within the bound.
No kernel may reach another device: no remote copies, remote signals or barrier semaphores. Data moves between devices by JAX's collectives and lax.ppermute only.
A program may use at most 128 MiB of HBM per device.

```python
import jax
import jax.numpy as jnp
from jax import lax

C = 640
HEAD_DIM = 64
W = 32
H = 32
FRAMES = 8
VIDEOS = 8


def draw_qkv_weight(key, part):
    key = jax.random.fold_in(key, 11)
    drawn = jnp.clip(jax.random.normal(key, (C, 3 * C), jnp.float32), -6.0, 6.0) * C ** (-0.5)
    return drawn.astype(jnp.bfloat16)


def with_spikes(array, key, source, target, blocks, factor):
    def block_of(axis_at):
        return (jnp.arange(array.shape[axis_at]) // (array.shape[axis_at] // blocks)).reshape((-1,) + (1,) * (array.ndim - 1 - axis_at))

    one_side = jax.random.permutation(key, blocks)[block_of(target)]
    far = (block_of(target) + blocks // 2) % blocks
    return jnp.where((block_of(source) == one_side) | (block_of(source) == far), factor * array, array)


def steps_of(stream_key, shape, shards, low, largest):
    def one(axis_at, shards_of):
        steps = jax.random.uniform(jax.random.fold_in(jax.random.fold_in(stream_key, 6), axis_at), (shards_of,), jnp.float32, low / len(shards), largest / len(shards))
        return jnp.repeat(jnp.exp(steps), shape[axis_at] // shards_of).reshape((-1,) + (1,) * (len(shape) - axis_at - 1))

    level = one(*shards[0])
    for cut in shards[1:]:
        level = level * one(*cut)
    return level


def centred(key, extent, width, limit, split=(), dtype=jnp.bfloat16):
    entries = jax.random.normal(key, extent, jnp.float32) * width
    if len(split) > 0:
        entries = steps_of(key, extent, split, -0.22, 0.18) * entries
    return jnp.clip(entries, min=-limit, max=limit).astype(dtype)


def noise_with(stream_key, dims, scale, most, pieces, heavy, dtype=jnp.bfloat16):
    values = scale * jax.random.normal(stream_key, dims, jnp.float32)
    if pieces:
        values = values * steps_of(stream_key, dims, pieces, -0.22, 0.18)
    return jnp.clip(with_spikes(values, jax.random.fold_in(stream_key, 3), *heavy), -most, most).astype(dtype)


def setup_inputs(seed: int = 0) -> dict:
    streams_of = jax.random.split(jax.random.key(seed), 8)
    return {
        "latents": centred(streams_of[0], (VIDEOS, FRAMES, H, W, C), 1.0, 6.0, ((0, 8), (1, 8), (2, 4))),
        "space_kernel": centred(streams_of[1], (3, 3, C, C), (9 * C) ** -0.5, 0.078125),
        "time_kernel": centred(streams_of[2], (3 * C, C), (3 * C) ** -0.5, 0.125, ((0, 8),)),
        "qkv_weight": draw_qkv_weight(jax.random.fold_in(streams_of[7], 71), 0),
        "out_weight": centred(streams_of[4], (C, C), C ** -0.5, 0.25, ((0, 8),)),
        "norm_gain": jnp.clip(1.0 + 0.15 * jax.random.normal(streams_of[5], (C,), jnp.float32), 0.25, 1.75),
        "grad_out": noise_with(streams_of[6], (VIDEOS, FRAMES, H, W, C), 1.0, 6.0, ((0, 8), (1, 8), (2, 4)), (1, 4, 8, 2.0)),
    }


def correlate(images, kernel, padding):
    return lax.conv_general_dilated(images, kernel, (1, 1), padding, dimension_numbers=('NHWC', 'HWIO', 'NHWC'), preferred_element_type=jnp.float32)

def flat_dot(former, latter):
    former_dims = former.shape
    result = jnp.dot(former.reshape(-1, former_dims[-1]), latter, preferred_element_type=jnp.float32)
    return result.reshape(former_dims[:-1] + (latter.shape[-1],))

def outer_sum(former, latter):
    return lax.dot_general(former.reshape(-1, former.shape[-1]), latter.reshape(-1, latter.shape[-1]), (((0,), (0,)), ((), ())), preferred_element_type=jnp.float32)

def stacked(activated):
    padded = jnp.pad(activated, ((1, 1), (0, 0), (0, 0)))
    return jnp.concatenate([padded[:-2], padded[1:-1], padded[2:]], axis=-1)

def normed(values, norm_gain):
    return values * lax.rsqrt(lax.optimization_barrier(jnp.mean(values * values, axis=-1, keepdims=True)) + 1e-06) * norm_gain

def temporal_mix(packed):
    frames_n, pixels, triple = packed.shape
    channels = triple // 3
    head_count = channels // HEAD_DIM
    split_up = packed.astype(jnp.float32).reshape(frames_n, pixels, 3, head_count, HEAD_DIM)
    queries = split_up[:, :, 0]
    key_part = split_up[:, :, 1]
    value_part = split_up[:, :, 2]
    scores = jnp.einsum('fpnd,gpnd->pnfg', queries, key_part) * HEAD_DIM ** (-0.5)
    scores = scores - lax.optimization_barrier(jnp.max(scores, axis=-1, keepdims=True))
    expons = jnp.exp(scores)
    probs = expons / lax.optimization_barrier(jnp.sum(expons, axis=-1, keepdims=True))
    probs = lax.optimization_barrier(probs.astype(jnp.bfloat16)).astype(jnp.float32)
    blended = jnp.einsum('pnfg,gpnd->fpnd', probs, value_part)
    return blended.reshape(frames_n, pixels, channels).astype(jnp.bfloat16)

def tile_backward(spatial, incoming, time_kernel, qkv_weight, out_weight, norm_gain):
    as_float = spatial.astype(jnp.float32)
    activated = jax.nn.silu(as_float).astype(jnp.bfloat16)
    stacked_in = stacked(activated)
    temporal = (as_float + flat_dot(stacked_in, time_kernel)).astype(jnp.bfloat16)
    temporal_f = temporal.astype(jnp.float32)
    normal_in = normed(temporal_f, norm_gain).astype(jnp.bfloat16)
    packed = flat_dot(normal_in, qkv_weight).astype(jnp.bfloat16)
    blended, mix_back = jax.vjp(temporal_mix, packed)
    grad_outproj = outer_sum(blended, incoming)
    grad_blend = flat_dot(incoming, out_weight.T).astype(jnp.bfloat16)
    grad_packed = mix_back(grad_blend)[0]
    grad_qkv = outer_sum(normal_in, grad_packed)
    grad_normal = flat_dot(grad_packed, qkv_weight.T)
    normal_f, norm_back = jax.vjp(lambda values: normed(values, norm_gain), temporal_f)
    grad_temporal = (incoming.astype(jnp.float32) + norm_back(grad_normal)[0]).astype(jnp.bfloat16)
    grad_stack = flat_dot(grad_temporal, time_kernel.T)
    channels = grad_stack.shape[-1] // 3
    grad_act = grad_stack[..., channels:2 * channels]
    grad_act = grad_act + jnp.pad(grad_stack[1:, :, :channels], ((0, 1), (0, 0), (0, 0)))
    grad_act = grad_act + jnp.pad(grad_stack[:-1, :, 2 * channels:], ((1, 0), (0, 0), (0, 0)))
    logistic = jax.nn.sigmoid(as_float)
    grad_spatial = (grad_temporal.astype(jnp.float32) + grad_act * logistic * (1.0 + as_float * (1.0 - logistic))).astype(jnp.bfloat16)
    return (grad_spatial, grad_qkv, grad_outproj)

def reference(latents, space_kernel, time_kernel, qkv_weight, out_weight, norm_gain, grad_out):
    videos, frames_n, height, cols_n, channels = latents.shape
    images = latents.reshape(-1, height, cols_n, channels)
    spatial = (images.astype(jnp.float32) + correlate(images, space_kernel, [(1, 1), (1, 1)])).astype(jnp.bfloat16)
    spatial = spatial.reshape(videos, frames_n, height * cols_n, channels)
    incoming = grad_out.reshape(videos, frames_n, height * cols_n, channels)

    def one_video(paired):
        return tile_backward(paired[0], paired[1], time_kernel, qkv_weight, out_weight, norm_gain)
    grad_spatial, grad_qkv, grad_outproj = lax.map(one_video, (spatial, incoming))
    grad_spatial = grad_spatial.reshape(-1, height, cols_n, channels)
    flipped = jnp.flip(space_kernel, (0, 1)).transpose(0, 1, 3, 2)
    grad_latents = (grad_spatial.astype(jnp.float32) + correlate(grad_spatial, flipped, [(1, 1), (1, 1)])).astype(jnp.bfloat16)
    grad_latents = grad_latents.reshape(latents.shape)
    return (grad_latents, lax.optimization_barrier(jnp.sum(grad_qkv, axis=0)), lax.optimization_barrier(jnp.sum(grad_outproj, axis=0)))
```

```python
import functools

import jax
import jax.numpy as jnp
from jax import lax
from jax.experimental import pallas as pl
from jax.experimental.pallas import tpu as pltpu
from jax.sharding import Mesh
from jax.sharding import PartitionSpec as P

HEAD_DIM = 64
C = 640
F32 = jnp.float32
BF16 = jnp.bfloat16
VIDEO = ("zl", "y")
FRAME = ("x", "c")
MIB = 1 << 20


def sds(shape, dtype=BF16):
    return jax.ShapeDtypeStruct(shape, dtype)


def call(body, outs, n_vmem, n_any, scratch=(), limit=48, flops=0, moved=0):
    specs = [pl.BlockSpec(memory_space=pltpu.SMEM)]
    specs += [pl.BlockSpec(memory_space=pltpu.VMEM)] * n_vmem
    specs += [pl.BlockSpec(memory_space=pl.ANY)] * n_any
    return pl.pallas_call(
        body,
        out_shape=outs,
        in_specs=specs,
        out_specs=[pl.BlockSpec(memory_space=pltpu.VMEM)] * len(outs),
        scratch_shapes=list(scratch),
        compiler_params=pltpu.CompilerParams(vmem_limit_bytes=limit * MIB),
        cost_estimate=pl.CostEstimate(flops=flops, bytes_accessed=moved, transcendentals=0),
    )


def position():
    return jnp.stack([lax.axis_index(n) for n in ("zl", "y", "x", "c", "zh")]).astype(jnp.int32)


def mm(a, b):
    return lax.dot_general(a, b, (((1,), (0,)), ((), ())), preferred_element_type=F32)


def mm_nt(a, b):
    return lax.dot_general(a, b, (((1,), (1,)), ((), ())), preferred_element_type=F32)


def mm_tn(a, b):
    return lax.dot_general(a, b, (((0,), (0,)), ((), ())), preferred_element_type=F32)


def shifted_columns(images_ref, low_ref, high_ref, zh, shifts_ref, order):
    low = low_ref[...].astype(F32) * jnp.where(zh > 0, 1.0, 0.0)
    high = high_ref[...].astype(F32) * jnp.where(zh < 3, 1.0, 0.0)
    whole = jnp.concatenate([low, images_ref[...].astype(F32), high], axis=0)
    flat = whole.reshape(320, C)
    column = lax.broadcasted_iota(jnp.int32, (320, C), 0) % 32
    before = jnp.where(column == 0, 0.0, pltpu.roll(flat, 1, 0))
    after = jnp.where(column == 31, 0.0, pltpu.roll(flat, 319, 0))
    views = (before, flat, after)
    for j, which in enumerate(order):
        shifts_ref[:, j * C : (j + 1) * C] = views[which].astype(BF16)


def kernel_copies(kernel_hbm, kernel_ref, sems):
    return [
        pltpu.make_async_copy(kernel_hbm.at[pl.ds(dy, 1)], kernel_ref.at[pl.ds(dy, 1)], sems.at[dy])
        for dy in range(3)
    ]


def conv_forward_body(pos, images, low, high, grad_out, kernel_hbm, *rest):
    outs, (kernel_ref, shifts, rows, sems) = rest[:8], rest[8:]
    copies = kernel_copies(kernel_hbm, kernel_ref, sems)
    for copy in copies:
        copy.start()
    shifted_columns(images, low, high, pos[4], shifts, (0, 1, 2))
    total = images[...].astype(F32).reshape(256, C)
    for dy in range(3):
        copies[dy].wait()
        taps = kernel_ref[dy].reshape(3 * C, C)
        total = total + mm(shifts[32 * dy : 32 * dy + 256, :], taps)
    rows[...] = total.astype(BF16).reshape(8, 32, C)
    frame = pos[2] * 2 + pos[3]
    for k in range(8):
        outs[k][0] = rows[frame ^ k]
        outs[k][1] = grad_out[frame ^ k]


def conv_backward_body(pos, images, low, high, kernel_hbm, out, kernel_ref, shifts, sems):
    copies = kernel_copies(kernel_hbm, kernel_ref, sems)
    for copy in copies:
        copy.start()
    shifted_columns(images, low, high, pos[4], shifts, (2, 1, 0))
    total = images[...].astype(F32).reshape(256, C)
    for dy in range(3):
        copies[dy].wait()
        at = 32 * (2 - dy)
        for dx in range(3):
            total = total + mm_nt(shifts[at : at + 256, dx * C : (dx + 1) * C], kernel_ref[dy, dx])
    out[...] = total.astype(BF16).reshape(8, 32, C)


CONV_SCRATCH = (pltpu.VMEM((3, 3, C, C), BF16), pltpu.VMEM((320, 3 * C), BF16))


def conv_forward(pos, images, low, high, grad_out, kernel):
    return call(
        conv_forward_body,
        [sds((2, 32, C))] * 8,
        4,
        1,
        CONV_SCRATCH + (pltpu.VMEM((8, 32, C), BF16), pltpu.SemaphoreType.DMA((3,))),
        flops=2 * 256 * 9 * C * C,
        moved=9 * C * C * 2,
    )(pos, images, low, high, grad_out, kernel)


def conv_backward(pos, images, low, high, kernel):
    return call(
        conv_backward_body,
        [sds((8, 32, C))],
        3,
        1,
        CONV_SCRATCH + (pltpu.SemaphoreType.DMA((3,)),),
        flops=2 * 256 * 9 * C * C,
        moved=9 * C * C * 2,
    )(pos, images, low, high, kernel)[0]


def gather_weight(shard):
    flip = [((zl, 1), (1 - zl, 1)) for zl in range(2)] + [((zl, 0), (zl, 0)) for zl in range(2)]
    flip = [(a[0] * 2 + a[1], b[0] * 2 + b[1]) for a, b in flip]
    own = lax.ppermute(shard, ("zl", "c"), flip)

    def turn(sign):
        pairs = []
        for y in range(4):
            pairs.append((y * 2, (y + sign) % 4 * 2))
            pairs.append((y * 2 + 1, (y - sign) % 4 * 2 + 1))
        return pairs

    ahead = lax.ppermute(own, ("y", "c"), turn(1))
    behind = lax.ppermute(own, ("y", "c"), turn(-1))
    far = lax.ppermute(ahead, ("y", "c"), turn(1))
    mine = [own, ahead, behind, far]
    swap = [(0, 1), (1, 0)]
    return mine + [lax.ppermute(piece, "c", swap) for piece in mine]


def weight_copies(pos, pieces, target, rows, sem):
    zl, y, core = pos[0], pos[1], pos[3]
    copies = []
    for i, piece in enumerate(pieces):
        holder = core if i < 4 else 1 - core
        step = 1 - 2 * holder
        shift = (0, -step, step, 2)[i % 4]
        block_zl = jnp.where(holder == 0, zl, 1 - zl)
        block = block_zl * 4 + (y + shift + 4) % 4
        start = pl.multiple_of(block * rows, 16)
        copies.append(pltpu.make_async_copy(piece, target.at[pl.ds(start, rows)], sem.at[i]))
    return copies


def temporal_body(pos, *refs):
    pieces, gain, time_pieces = refs[:8], refs[8], refs[9:17]
    temporal_out, normal_out, spatial_out, incoming_out = refs[17:21]
    time_ref, padded, sem = refs[21:]
    copies = weight_copies(pos, time_pieces, time_ref, 240, sem)
    for copy in copies:
        copy.start()
    frame = pos[2] * 2 + pos[3]
    for k in range(8):
        source = frame ^ k
        piece = pieces[k][0]
        spatial_out[source] = piece
        incoming_out[source] = pieces[k][1]
        value = piece.astype(F32)
        padded[source + 1] = (value * jax.nn.sigmoid(value)).astype(BF16)
    padded[0] = jnp.zeros((32, C), BF16)
    padded[9] = jnp.zeros((32, C), BF16)
    total = spatial_out[...].astype(F32).reshape(256, C)
    for copy in copies:
        copy.wait()
    for k in range(3):
        total = total + mm(padded[k : k + 8].reshape(256, C), time_ref[k * C : (k + 1) * C, :])
    temporal = total.astype(BF16)
    temporal_out[...] = temporal
    value = temporal.astype(F32)
    scale = lax.rsqrt(jnp.mean(value * value, axis=-1, keepdims=True) + 1e-06)
    normal_out[...] = (value * scale * gain[...]).astype(BF16)


def temporal_step(pos, pieces, gain, time_pieces):
    return call(
        temporal_body,
        [sds((256, C)), sds((256, C)), sds((8, 32, C)), sds((8, 32, C))],
        9,
        8,
        (
            pltpu.VMEM((3 * C, C), BF16),
            pltpu.VMEM((10, 32, C), BF16),
            pltpu.SemaphoreType.DMA((8,)),
        ),
        flops=2 * 256 * 3 * C * C,
        moved=3 * C * C * 2,
    )(pos, *pieces, gain, *time_pieces)


def attention_body(pos, normal, incoming, *refs):
    weight_pieces, (grad_packed, keep, send) = refs[:8], refs[8:11]
    weight, packed, grad_blend, blended, sem = refs[11:]
    copies = weight_copies(pos, weight_pieces, weight, 80, sem)
    for copy in copies:
        copy.start()
    for copy in copies:
        copy.wait()
    packed[...] = mm(normal[...], weight[:, : 3 * C]).astype(BF16).reshape(8, 2, 16, 3 * C)
    arriving = incoming[...].reshape(256, C)
    grad_blend[...] = mm_nt(arriving, weight[:, 3 * C :]).astype(BF16).reshape(8, 2, 16, C)
    first_head = lax.broadcasted_iota(jnp.int32, (128, 128), 1) < HEAD_DIM
    row_pixel = lax.broadcasted_iota(jnp.int32, (256, 128), 0) % 16
    column_pixel = lax.broadcasted_iota(jnp.int32, (256, 128), 1) % 16
    same_pixel = row_pixel == column_pixel
    nothing = jnp.zeros((128, 128), BF16)

    def two_heads(block):
        return jnp.concatenate(
            [jnp.where(first_head, block, nothing), jnp.where(first_head, nothing, block)], axis=0
        )

    def merged(both):
        return jnp.where(first_head, both[:128], both[128:]).astype(BF16)

    for half in range(2):
        for pair in range(5):
            at = pair * 128

            def part(ref, offset):
                return ref[:, half, :, offset + at : offset + at + 128].reshape(128, 128)

            queries = two_heads(part(packed, 0))
            keys = part(packed, C)
            values = part(packed, 2 * C)
            scores = jnp.where(same_pixel, mm_nt(queries, keys) * HEAD_DIM**-0.5, -1e30)
            expons = jnp.exp(scores - jnp.max(scores, axis=-1, keepdims=True))
            probs = expons * (1.0 / jnp.sum(expons, axis=-1, keepdims=True))
            rounded = probs.astype(BF16)
            blended[:, half, :, at : at + 128] = merged(mm(rounded, values)).reshape(8, 16, 128)
            upper = two_heads(part(grad_blend, 0))
            grad_probs = mm_nt(upper, values)
            inner = jnp.sum(grad_probs * probs, axis=-1, keepdims=True)
            grad_scores = (probs * (grad_probs - inner) * HEAD_DIM**-0.5).astype(BF16)
            results = (
                merged(mm(grad_scores, keys)),
                mm_tn(grad_scores, queries).astype(BF16),
                mm_tn(rounded, upper).astype(BF16),
            )
            for i, result in enumerate(results):
                lanes = slice(i * C + at, i * C + at + 128)
                grad_packed[:, half, :, lanes] = result.reshape(8, 16, 128)

    core = pos[3]
    whole = grad_packed[...].reshape(256, 3 * C)

    def columns(array, width, which):
        starts = [(2 * x + which) * width for x in range(4)]
        return jnp.concatenate([array[:, s : s + width] for s in starts], axis=1)

    mixed = blended[...].reshape(256, C)
    qkv_parts = [columns(whole, 240, which) for which in range(2)]
    out_parts = [columns(arriving, 80, which) for which in range(2)]
    for target, swap in ((send, 0), (keep, 1)):
        first = core == swap
        qkv_side = jnp.where(first, qkv_parts[1], qkv_parts[0])
        out_side = jnp.where(first, out_parts[1], out_parts[0])
        target[:, 0:960] = mm_tn(normal[...], qkv_side).astype(BF16)
        target[:, 960:1280] = mm_tn(mixed, out_side).astype(BF16)


def attention_step(pos, normal, incoming, weight_pieces):
    return call(
        attention_body,
        [sds((8, 2, 16, 3 * C)), sds((C, 1280)), sds((C, 1280))],
        2,
        8,
        (
            pltpu.VMEM((C, 4 * C), BF16),
            pltpu.VMEM((8, 2, 16, 3 * C), BF16),
            pltpu.VMEM((8, 2, 16, C), BF16),
            pltpu.VMEM((8, 2, 16, C), BF16),
            pltpu.SemaphoreType.DMA((8,)),
        ),
        flops=2 * 256 * 10 * C * C,
        moved=4 * C * C * 2,
    )(pos, normal, incoming, *weight_pieces)


def tile_gradient_body(pos, *refs):
    grad_packed, temporal, incoming, spatial, gain = refs[:5]
    weight_pieces, time_pieces, outs = refs[5:13], refs[13:21], refs[21:29]
    weight, time_ref, padded, rows, sem, time_sem = refs[29:]
    copies = weight_copies(pos, weight_pieces, weight, 80, sem)
    time_copies = weight_copies(pos, time_pieces, time_ref, 240, time_sem)
    for copy in copies + time_copies:
        copy.start()
    for copy in copies:
        copy.wait()
    grad_normal = mm_nt(grad_packed[...].reshape(256, 3 * C), weight[:, : 3 * C])
    value = temporal[...].astype(F32)
    scale = lax.rsqrt(jnp.mean(value * value, axis=-1, keepdims=True) + 1e-06)
    scaled = grad_normal * gain[...]
    inner = jnp.mean(value * scaled, axis=-1, keepdims=True)
    through_norm = scale * scaled - value * (scale * scale * scale * inner)
    grad_temporal = (incoming[...].astype(F32).reshape(256, C) + through_norm).astype(BF16)
    padded[0] = jnp.zeros((32, C), BF16)
    padded[1:9] = grad_temporal.reshape(8, 32, C)
    padded[9] = jnp.zeros((32, C), BF16)
    for copy in time_copies:
        copy.wait()
    grad_act = jnp.zeros((256, C), F32)
    for k in range(3):
        later = padded[2 - k : 10 - k].reshape(256, C)
        grad_act = grad_act + mm_nt(later, time_ref[k * C : (k + 1) * C, :])
    as_float = spatial[...].astype(F32).reshape(256, C)
    logistic = jax.nn.sigmoid(as_float)
    grad_spatial = grad_temporal.astype(F32) + grad_act * logistic * (
        1.0 + as_float * (1.0 - logistic)
    )
    rows[...] = grad_spatial.astype(BF16).reshape(8, 32, C)
    frame = pos[2] * 2 + pos[3]
    for k in range(8):
        outs[k][...] = rows[frame ^ k]


def tile_gradient(pos, grad_packed, temporal, incoming, spatial, gain, weights, times):
    return call(
        tile_gradient_body,
        [sds((32, C))] * 8,
        5,
        16,
        (
            pltpu.VMEM((C, 4 * C), BF16),
            pltpu.VMEM((3 * C, C), BF16),
            pltpu.VMEM((10, 32, C), BF16),
            pltpu.VMEM((8, 32, C), BF16),
            pltpu.SemaphoreType.DMA((8,)),
            pltpu.SemaphoreType.DMA((8,)),
        ),
        flops=2 * 256 * 6 * C * C,
        moved=7 * C * C * 2,
    )(pos, grad_packed, temporal, incoming, spatial, gain, *weights, *times)


def frame_rows_body(pos, *refs):
    pieces, (rows, top, bottom) = refs[:8], refs[8:]
    frame = pos[2] * 2 + pos[3]
    for k in range(8):
        rows[frame ^ k] = pieces[k][...]
    top[...] = rows[0:1]
    bottom[...] = rows[7:8]


def frame_rows(pos, pieces):
    outs = [sds((8, 32, C)), sds((1, 32, C)), sds((1, 32, C))]
    return call(frame_rows_body, outs, 8, 0, moved=4 * 256 * C)(pos, *pieces)


def pair_sum_body(pos, keep, other, own, *sends):
    y = pos[1]

    def block(index):
        return keep[:, index].astype(F32) + other[:, index].astype(F32)

    own[...] = block(y)
    for k in range(3):
        sends[k][...] = block((y + k + 1) % 4).astype(BF16)


def video_sum_body(pos, held, *refs):
    others, own, sends, scratch = refs[:3], refs[3], refs[4:7], refs[7]
    total = held[...]
    for other in others:
        total = total + other[...].astype(F32)
    for x in range(4):
        scratch[x, :, :, 0:240] = total[:, :, 240 * x : 240 * x + 240]
        scratch[x, :, :, 240:320] = total[:, :, 960 + 80 * x : 960 + 80 * x + 80]
    own[...] = scratch[pos[2]]
    for k in range(3):
        sends[k][...] = scratch[(pos[2] + k + 1) % 4].astype(BF16)


def frame_sum_body(pos, held, *refs):
    others, own, sends, scratch = refs[:3], refs[3], refs[4:7], refs[7]
    total = held[...]
    for other in others:
        total = total + other[...].astype(F32)
    for row in range(4):
        scratch[row, :, :, 0:60] = total[:, :, 60 * row : 60 * row + 60]
        scratch[row, :, :, 60:80] = total[:, :, 240 + 20 * row : 240 + 20 * row + 20]
    own[...] = scratch[pos[4]]
    for k in range(3):
        sends[k][...] = scratch[(pos[4] + k + 1) % 4].astype(BF16)


def row_sum_body(pos, held, *refs):
    others, (own, send, scratch) = refs[:3], refs[3:]
    total = held[...]
    for other in others:
        total = total + other[...].astype(F32)
    scratch[...] = total
    own[...] = scratch[pos[0]]
    send[...] = scratch[1 - pos[0]].astype(BF16)


def last_sum_body(pos, held, other, qkv_out, out_out):
    total = held[...] + other[...].astype(F32)
    qkv_out[...] = total[:, 0:60]
    out_out[...] = total[:, 60:80]


def round_trip(sends, axis):
    return [
        lax.ppermute(sends[k], axis, [(i, (i + k + 1) % 4) for i in range(4)]) for k in range(3)
    ]


def reduce_grads(pos, keep, send):
    other = lax.ppermute(send, "c", [(0, 1), (1, 0)])
    shape = (2, 4, 80, 1280)
    step = (2, 80, 1280)
    own, *sends = call(pair_sum_body, [sds(step, F32)] + [sds(step)] * 3, 2, 0)(
        pos, keep.reshape(shape), other.reshape(shape)
    )
    step = (2, 80, 320)
    own, *sends = call(
        video_sum_body,
        [sds(step, F32)] + [sds(step)] * 3,
        4,
        0,
        (pltpu.VMEM((4,) + step, F32),),
    )(pos, own, *round_trip(sends, "y"))
    step = (2, 80, 80)
    own, *sends = call(
        frame_sum_body,
        [sds(step, F32)] + [sds(step)] * 3,
        4,
        0,
        (pltpu.VMEM((4,) + step, F32),),
    )(pos, own, *round_trip(sends, "x"))
    own, send = call(
        row_sum_body, [sds((80, 80), F32), sds((80, 80))], 4, 0, (pltpu.VMEM(step, F32),)
    )(pos, own, *round_trip(sends, "zh"))
    other = lax.ppermute(send, "zl", [(0, 1), (1, 0)])
    return call(last_sum_body, [sds((80, 60), F32), sds((80, 20), F32)], 2, 0)(pos, own, other)


def edges(top, bottom):
    low = lax.ppermute(bottom, "zh", [(i, (i + 1) % 4) for i in range(4)])
    high = lax.ppermute(top, "zh", [(i, (i + 3) % 4) for i in range(4)])
    return low, high


def spread(pieces):
    out = [pieces[0]]
    for k in range(1, 8):
        out.append(lax.ppermute(pieces[k], FRAME, [(i, i ^ k) for i in range(8)]))
    return out


def shards(latents, space_kernel, time_kernel, qkv_weight, out_weight, norm_gain, grad_out):
    pos = position()
    images, incoming = latents[0, 0], grad_out[0, 0]
    gain = norm_gain.reshape(1, C)
    low, high = edges(images[0:1], images[7:8])
    times = gather_weight(time_kernel)
    weights = gather_weight(jnp.concatenate([qkv_weight, out_weight], axis=1))
    pieces = spread(conv_forward(pos, images, low, high, incoming, space_kernel))
    temporal, normal, spatial_tile, incoming_tile = temporal_step(pos, pieces, gain, times)
    grad_packed, keep, send = attention_step(pos, normal, incoming_tile, weights)
    rows = tile_gradient(
        pos, grad_packed, temporal, incoming_tile, spatial_tile, gain, weights, times
    )
    grad_spatial, top, bottom = frame_rows(pos, spread(rows))
    low, high = edges(top, bottom)
    grad_latents = conv_backward(pos, grad_spatial, low, high, space_kernel)
    grad_qkv, grad_outproj = reduce_grads(pos, keep, send)
    return grad_latents[None, None], grad_qkv, grad_outproj


def solution(mesh):
    inner = Mesh(mesh.devices.reshape(2, 4, 4, 2, 4), ("zl", "y", "x", "c", "zh"))
    tiles = P(VIDEO, FRAME, "zh", None, None)
    weight = P(VIDEO, None)
    grads = P(VIDEO, ("x", "c", "zh"))
    return jax.shard_map(
        shards,
        mesh=inner,
        in_specs=(tiles, P(), weight, weight, weight, P(), tiles),
        out_specs=(tiles, grads, grads),
        check_vma=False,
    )
```

```python
import functools

import jax
import jax.numpy as jnp
from jax import lax
from jax.experimental import pallas as pl
from jax.experimental.pallas import tpu as pltpu
from jax.sharding import Mesh
from jax.sharding import PartitionSpec as P

HEAD_DIM = 64
C = 640
F32 = jnp.float32
BF16 = jnp.bfloat16
VIDEO = ("zl", "y")
FRAME = ("x", "c")
MIB = 1 << 20


def sds(shape, dtype=BF16):
    return jax.ShapeDtypeStruct(shape, dtype)


AXES = ("zl", "y", "x", "c", "zh")


def call(body, outs, n_vmem, n_any, scratch=(), limit=12, flops=0, moved=0):
    def placed_body(*refs):
        body([lax.axis_index(name) for name in AXES], *refs)

    specs = [pl.BlockSpec(memory_space=pltpu.VMEM)] * n_vmem
    specs += [pl.BlockSpec(memory_space=pl.ANY)] * n_any
    return pl.pallas_call(
        placed_body,
        out_shape=outs,
        in_specs=specs,
        out_specs=[pl.BlockSpec(memory_space=pltpu.VMEM)] * len(outs),
        scratch_shapes=list(scratch),
        compiler_params=pltpu.CompilerParams(vmem_limit_bytes=limit * MIB),
        cost_estimate=pl.CostEstimate(flops=flops, bytes_accessed=moved, transcendentals=0),
    )


def mm(a, b):
    return lax.dot_general(a, b, (((1,), (0,)), ((), ())), preferred_element_type=F32)


def mm_nt(a, b):
    return lax.dot_general(a, b, (((1,), (1,)), ((), ())), preferred_element_type=F32)


def mm_tn(a, b):
    return lax.dot_general(a, b, (((0,), (0,)), ((), ())), preferred_element_type=F32)


def shifted_columns(images_ref, low_ref, high_ref, zh, shifts_ref, order):
    low = low_ref[...].astype(F32) * jnp.where(zh > 0, 1.0, 0.0)
    high = high_ref[...].astype(F32) * jnp.where(zh < 3, 1.0, 0.0)
    whole = jnp.concatenate([low, images_ref[...].astype(F32), high], axis=0)
    flat = whole.reshape(320, C)
    column = lax.broadcasted_iota(jnp.int32, (320, C), 0) % 32
    before = jnp.where(column == 0, 0.0, pltpu.roll(flat, 1, 0))
    after = jnp.where(column == 31, 0.0, pltpu.roll(flat, 319, 0))
    views = (before, flat, after)
    for j, which in enumerate(order):
        shifts_ref[:, j * C : (j + 1) * C] = views[which].astype(BF16)


def kernel_copies(kernel_hbm, kernel_ref, sems):
    return [
        pltpu.make_async_copy(kernel_hbm.at[pl.ds(dy, 1)], kernel_ref.at[pl.ds(dy, 1)], sems.at[dy])
        for dy in range(3)
    ]


def conv_forward_body(pos, images, low, high, grad_out, kernel_hbm, out, *rest):
    kernel_ref, shifts, sems = rest
    copies = kernel_copies(kernel_hbm, kernel_ref, sems)
    for copy in copies:
        copy.start()
    shifted_columns(images, low, high, pos[4], shifts, (0, 1, 2))
    total = images[...].astype(F32).reshape(256, C)
    for dy in range(3):
        copies[dy].wait()
        taps = kernel_ref[dy].reshape(3 * C, C)
        total = total + mm(shifts[32 * dy : 32 * dy + 256, :], taps)
    out[:, 0] = total.astype(BF16).reshape(8, 32, C)
    out[:, 1] = grad_out[...]


def conv_backward_body(pos, images, low, high, kernel_hbm, out, token, kernel_ref, shifts, sems):
    token[...] = jnp.zeros((8, 128), F32)
    copies = kernel_copies(kernel_hbm, kernel_ref, sems)
    for copy in copies:
        copy.start()
    shifted_columns(images, low, high, pos[4], shifts, (2, 1, 0))
    total = images[...].astype(F32).reshape(256, C)
    for dy in range(3):
        copies[dy].wait()
        at = 32 * (2 - dy)
        for dx in range(3):
            total = total + mm_nt(shifts[at : at + 256, dx * C : (dx + 1) * C], kernel_ref[dy, dx])
    out[...] = total.astype(BF16).reshape(8, 32, C)


CONV_SCRATCH = (pltpu.VMEM((3, 3, C, C), BF16), pltpu.VMEM((320, 3 * C), BF16))


def conv_forward(images, low, high, grad_out, kernel):
    return call(
        conv_forward_body,
        [sds((8, 2, 32, C))],
        4,
        1,
        CONV_SCRATCH + (pltpu.SemaphoreType.DMA((3,)),),
        limit=48,
        flops=2 * 256 * 9 * C * C,
        moved=9 * C * C * 2,
    )(images, low, high, grad_out, kernel)[0]


def conv_backward(images, low, high, kernel):
    return call(
        conv_backward_body,
        [sds((8, 32, C)), sds((8, 128), F32)],
        3,
        1,
        CONV_SCRATCH + (pltpu.SemaphoreType.DMA((3,)),),
        limit=48,
        flops=2 * 256 * 9 * C * C,
        moved=9 * C * C * 2,
    )(images, low, high, kernel)


def half_body(pos, time, half, sem):
    rows = time.at[pl.ds(pl.multiple_of(112 * pos[3], 16), 128)]
    copy = pltpu.make_async_copy(rows, half, sem)
    copy.start()
    copy.wait()


def half_time(time):
    dma = (pltpu.SemaphoreType.DMA,)
    return call(half_body, [sds((128, C))], 0, 1, dma, limit=62)(time)[0]


def half_projections_body(pos, qkv, out, *refs):
    core, (half, sems) = pos[3], refs[3:]

    def run(first, second):
        copies = [
            pltpu.make_async_copy(first, half.at[0:80], sems.at[0]),
            pltpu.make_async_copy(second, half.at[80:160], sems.at[1]),
        ]
        for copy in copies:
            copy.start()
        for copy in copies:
            copy.wait()

    @pl.when(core == 0)
    def _():
        run(qkv.at[:, 0:C], qkv.at[:, C : 2 * C])

    @pl.when(core == 1)
    def _():
        run(qkv.at[:, 2 * C : 3 * C], out)


def half_projections(qkv, out, after):
    dma = (pltpu.SemaphoreType.DMA((2,)),)
    return call(half_projections_body, [sds((160, C))], 0, 5, dma, limit=62)(qkv, out, *after)[0]


def gate(value, after):
    return pl.pallas_call(
        lambda a, b, c: None,
        out_shape=sds(value.shape, value.dtype),
        in_specs=[pl.BlockSpec(memory_space=pl.ANY)] * 2,
        out_specs=pl.BlockSpec(memory_space=pl.ANY),
        input_output_aliases={0: 0},
    )(value, after)


def four_body(pos, own, *refs):
    others, out = refs[:3], refs[-1]
    out[pos[1]] = own[...]
    for k in range(3):
        out[(pos[1] + 3 - k) % 4] = others[k][...]


def four(own, others, after):
    return call(four_body, [sds((4,) + own.shape)], 4, 1)(own, *others, after)[0]


def across(own):
    pairs = []
    for z in range(8):
        for core in range(2):
            to = (z + 7 + 2 * core) % 8
            pairs.append(tuple(((at % 2) * 2 + core) * 4 + at // 2 for at in (z, to)))
    return lax.ppermute(own, ("zl", "c", "zh"), pairs)


def swapped(value):
    return lax.ppermute(value, "c", [(0, 1), (1, 0)])


def time_copies(pos, pieces, target, sem):
    zl, core = pos[0], pos[3]
    copies = []
    for i, piece in enumerate(pieces):
        blocks = pl.ds(4 * (zl if i % 2 == 0 else 1 - zl), 4)
        half = core if i < 2 else 1 - core
        source = piece.at[:, pl.ds(pl.multiple_of(16 * half, 16), 112)]
        place = target.at[blocks, pl.ds(pl.multiple_of(128 * half, 16), 112)]
        copies.append(pltpu.make_async_copy(source, place, sem.at[i]))
        if i < 2:
            source = piece.at[:, pl.ds(pl.multiple_of(112 * (1 - half), 16), 16)]
            place = target.at[blocks, pl.ds(112, 16)]
            copies.append(pltpu.make_async_copy(source, place, sem.at[4 + i]))
    return copies


def projection_copies(pos, pieces, target, sem):
    zl, core = pos[0], pos[3]
    copies = []
    for i, piece in enumerate(pieces):
        blocks = pl.ds(4 * (zl if i % 2 == 0 else 1 - zl), 4)
        half = core if i < 2 else 1 - core
        for j in range(2):
            lanes = pl.ds(pl.multiple_of(1280 * half + 640 * j, 128), 640)
            source = piece.at[:, 80 * j : 80 * j + 80]
            copies.append(pltpu.make_async_copy(source, target.at[blocks, :, lanes], sem.at[2 * i + j]))
    return copies


def gathered(own, after):
    far = gate(across(own), after)
    return [own, far, swapped(own), swapped(far)]


def temporal_body(pos, tile, gain, *refs):
    time_pieces, (temporal_out, normal_out) = refs[:4], refs[4:6]
    time_ref, padded, sem = refs[6:]
    copies = time_copies(pos, time_pieces, time_ref, sem)
    for copy in copies:
        copy.start()
    value = tile[:, 0].astype(F32)
    padded[0] = jnp.zeros((32, C), BF16)
    padded[1:9] = (value * jax.nn.sigmoid(value)).astype(BF16)
    padded[9] = jnp.zeros((32, C), BF16)
    total = value.reshape(256, C)
    for copy in copies:
        copy.wait()
    taps = time_ref[...].reshape(3 * C, C)
    for k in range(3):
        total = total + mm(padded[k : k + 8].reshape(256, C), taps[k * C : (k + 1) * C, :])
    temporal = total.astype(BF16)
    temporal_out[...] = temporal
    value = temporal.astype(F32)
    scale = lax.rsqrt(jnp.mean(value * value, axis=-1, keepdims=True) + 1e-06)
    normal_out[...] = (value * scale * gain[...]).astype(BF16)


TIME_SCRATCH = (pltpu.VMEM((8, 240, C), BF16), pltpu.VMEM((10, 32, C), BF16))


def temporal_step(tile, gain, time_pieces):
    return call(
        temporal_body,
        [sds((256, C)), sds((256, C))],
        2,
        4,
        TIME_SCRATCH + (pltpu.SemaphoreType.DMA((6,)),),
        limit=20,
        flops=2 * 256 * 3 * C * C,
        moved=3 * C * C * 2,
    )(tile, gain, *time_pieces)


def attention_body(pos, normal, tile, *refs):
    weight_pieces, (grad_packed, keep, send) = refs[:4], refs[4:7]
    weight_ref, packed, grad_blend, blended, sem = refs[7:]
    copies = projection_copies(pos, weight_pieces, weight_ref, sem)
    for copy in copies:
        copy.start()
    for copy in copies:
        copy.wait()
    weight = weight_ref[...].reshape(C, 4 * C)
    packed[...] = mm(normal[...], weight[:, : 3 * C]).astype(BF16).reshape(8, 2, 16, 3 * C)
    arriving = tile[:, 1].reshape(256, C)
    grad_blend[...] = mm_nt(arriving, weight[:, 3 * C :]).astype(BF16).reshape(8, 2, 16, C)
    first_head = lax.broadcasted_iota(jnp.int32, (128, 128), 1) < HEAD_DIM
    row_pixel = lax.broadcasted_iota(jnp.int32, (256, 128), 0) % 16
    column_pixel = lax.broadcasted_iota(jnp.int32, (256, 128), 1) % 16
    same_pixel = row_pixel == column_pixel
    nothing = jnp.zeros((128, 128), BF16)

    def two_heads(block):
        return jnp.concatenate(
            [jnp.where(first_head, block, nothing), jnp.where(first_head, nothing, block)], axis=0
        )

    def merged(both):
        return jnp.where(first_head, both[:128], both[128:]).astype(BF16)

    for half in range(2):
        for pair in range(5):
            at = pair * 128

            def part(ref, offset):
                return ref[:, half, :, offset + at : offset + at + 128].reshape(128, 128)

            queries = two_heads(part(packed, 0))
            keys = part(packed, C)
            values = part(packed, 2 * C)
            scores = jnp.where(same_pixel, mm_nt(queries, keys) * HEAD_DIM**-0.5, -1e30)
            expons = jnp.exp(scores - jnp.max(scores, axis=-1, keepdims=True))
            probs = expons * (1.0 / jnp.sum(expons, axis=-1, keepdims=True))
            rounded = probs.astype(BF16)
            blended[:, half, :, at : at + 128] = merged(mm(rounded, values)).reshape(8, 16, 128)
            upper = two_heads(part(grad_blend, 0))
            grad_probs = mm_nt(upper, values)
            inner = jnp.sum(grad_probs * probs, axis=-1, keepdims=True)
            grad_scores = (probs * (grad_probs - inner) * HEAD_DIM**-0.5).astype(BF16)
            results = (
                merged(mm(grad_scores, keys)),
                mm_tn(grad_scores, queries).astype(BF16),
                mm_tn(rounded, upper).astype(BF16),
            )
            for i, result in enumerate(results):
                lanes = slice(i * C + at, i * C + at + 128)
                grad_packed[:, half, :, lanes] = result.reshape(8, 16, 128)

    core = pos[3]
    whole = grad_packed[...].reshape(256, 3 * C)

    def columns(array, width, which):
        starts = [(2 * x + which) * width for x in range(4)]
        return jnp.concatenate([array[:, s : s + width] for s in starts], axis=1)

    mixed = blended[...].reshape(256, C)
    qkv_parts = [columns(whole, 240, which) for which in range(2)]
    out_parts = [columns(arriving, 80, which) for which in range(2)]
    for target, swap in ((send, 0), (keep, 1)):
        first = core == swap
        qkv_side = jnp.where(first, qkv_parts[1], qkv_parts[0])
        out_side = jnp.where(first, out_parts[1], out_parts[0])
        target[:, 0:960] = mm_tn(normal[...], qkv_side).astype(BF16)
        target[:, 960:1280] = mm_tn(mixed, out_side).astype(BF16)


def attention_step(normal, tile, weight_pieces):
    return call(
        attention_body,
        [sds((8, 2, 16, 3 * C)), sds((C, 1280)), sds((C, 1280))],
        2,
        4,
        (
            pltpu.VMEM((8, 80, 4 * C), BF16),
            pltpu.VMEM((8, 2, 16, 3 * C), BF16),
            pltpu.VMEM((8, 2, 16, C), BF16),
            pltpu.VMEM((8, 2, 16, C), BF16),
            pltpu.SemaphoreType.DMA((8,)),
        ),
        limit=36,
        flops=2 * 256 * 10 * C * C,
        moved=4 * C * C * 2,
    )(normal, tile, *weight_pieces)


def tile_gradient_body(pos, *refs):
    grad_packed, temporal, tile, gain = refs[:4]
    weight_pieces, time_pieces, out = refs[4:8], refs[8:12], refs[13]
    weight_ref, time_ref, padded, sem, time_sem = refs[14:]
    copies = projection_copies(pos, weight_pieces, weight_ref, sem)
    later_copies = time_copies(pos, time_pieces, time_ref, time_sem)
    for copy in copies + later_copies:
        copy.start()
    for copy in copies:
        copy.wait()
    weight = weight_ref[...].reshape(C, 4 * C)[:, : 3 * C]
    grad_normal = mm_nt(grad_packed[...].reshape(256, 3 * C), weight)
    value = temporal[...].astype(F32)
    scale = lax.rsqrt(jnp.mean(value * value, axis=-1, keepdims=True) + 1e-06)
    scaled = grad_normal * gain[...]
    inner = jnp.mean(value * scaled, axis=-1, keepdims=True)
    through_norm = scale * scaled - value * (scale * scale * scale * inner)
    grad_temporal = (tile[:, 1].astype(F32).reshape(256, C) + through_norm).astype(BF16)
    padded[0] = jnp.zeros((32, C), BF16)
    padded[1:9] = grad_temporal.reshape(8, 32, C)
    padded[9] = jnp.zeros((32, C), BF16)
    for copy in later_copies:
        copy.wait()
    taps = time_ref[...].reshape(3 * C, C)
    grad_act = jnp.zeros((256, C), F32)
    for k in range(3):
        later = padded[2 - k : 10 - k].reshape(256, C)
        grad_act = grad_act + mm_nt(later, taps[k * C : (k + 1) * C, :])
    as_float = tile[:, 0].astype(F32).reshape(256, C)
    logistic = jax.nn.sigmoid(as_float)
    grad_spatial = grad_temporal.astype(F32) + grad_act * logistic * (
        1.0 + as_float * (1.0 - logistic)
    )
    out[...] = grad_spatial.astype(BF16).reshape(8, 32, C)


def tile_gradient(grad_packed, temporal, tile, gain, weights, times, after):
    return call(
        tile_gradient_body,
        [sds((8, 32, C))],
        4,
        9,
        (pltpu.VMEM((8, 80, 4 * C), BF16),)
        + TIME_SCRATCH
        + (pltpu.SemaphoreType.DMA((8,)), pltpu.SemaphoreType.DMA((6,))),
        limit=28,
        flops=2 * 256 * 6 * C * C,
        moved=7 * C * C * 2,
    )(grad_packed, temporal, tile, gain, *weights, *times, after)[0]


def pair_sum_body(pos, keep, other, own, *sends):
    y = pos[1]

    def block(index):
        return keep[:, index].astype(F32) + other[:, index].astype(F32)

    own[...] = block(y)
    for k in range(3):
        sends[k][...] = block((y + k + 1) % 4).astype(BF16)


def video_sum_body(pos, held, *refs):
    others, own, sends, scratch = refs[:3], refs[3], refs[4:7], refs[7]
    total = held[...]
    for other in others:
        total = total + other[...].astype(F32)
    for x in range(4):
        scratch[x, :, :, 0:240] = total[:, :, 240 * x : 240 * x + 240]
        scratch[x, :, :, 240:320] = total[:, :, 960 + 80 * x : 960 + 80 * x + 80]
    own[...] = scratch[pos[2]]
    for k in range(3):
        sends[k][...] = scratch[(pos[2] + k + 1) % 4].astype(BF16)


def frame_sum_body(pos, held, first, second, third, out):
    total = held[...]
    for other in (first, second, third):
        total = total + other[...].astype(F32)
    for row in range(4):
        out[row, :, :, 0:60] = total[:, :, 60 * row : 60 * row + 60].astype(BF16)
        out[row, :, :, 60:80] = total[:, :, 240 + 20 * row : 240 + 20 * row + 20].astype(BF16)


def row_sum_body(pos, parts, after, own, send, scratch):
    scratch[...] = jnp.sum(parts[...].astype(F32), axis=0)
    own[...] = scratch[pos[0]]
    send[...] = scratch[1 - pos[0]].astype(BF16)


def last_sum_body(pos, held, other, qkv_out, out_out):
    total = held[...] + other[...].astype(F32)
    qkv_out[...] = total[:, 0:60]
    out_out[...] = total[:, 60:80]


def round_trip(sends, axis):
    return [
        lax.ppermute(sends[k], axis, [(i, (i + k + 1) % 4) for i in range(4)]) for k in range(3)
    ]


def pair_sum(keep, send):
    shape = (2, 4, 80, 1280)
    step = (2, 80, 1280)
    return call(pair_sum_body, [sds(step, F32)] + [sds(step)] * 3, 2, 0, limit=20)(
        keep.reshape(shape), swapped(send).reshape(shape)
    )


def reduce_grads(own, sends, after):
    step = (2, 80, 320)
    own, *sends = call(
        video_sum_body,
        [sds(step, F32)] + [sds(step)] * 3,
        4,
        0,
        (pltpu.VMEM((4,) + step, F32),),
        limit=20,
    )(own, *round_trip(sends, "y"))
    parts = call(frame_sum_body, [sds((4, 2, 80, 80))], 4, 0)(
        own, *round_trip(sends, "x")
    )[0]
    parts = lax.all_to_all(parts, "zh", split_axis=0, concat_axis=0, tiled=True)
    own, send = call(
        row_sum_body, [sds((80, 80), F32), sds((80, 80))], 1, 1, (pltpu.VMEM((2, 80, 80), F32),)
    )(parts, after)
    other = lax.ppermute(send, "zl", [(0, 1), (1, 0)])
    return call(last_sum_body, [sds((80, 60), F32), sds((80, 20), F32)], 2, 0)(own, other)


def edges(images):
    low = lax.ppermute(images[7:8], "zh", [(i, (i + 1) % 4) for i in range(4)])
    high = lax.ppermute(images[0:1], "zh", [(i, (i + 3) % 4) for i in range(4)])
    return low, high


def exchange(rows):
    return lax.all_to_all(rows, FRAME, split_axis=0, concat_axis=0, tiled=True)


def shards(latents, space_kernel, time_kernel, qkv_weight, out_weight, norm_gain, grad_out):
    images, incoming = latents[0, 0], grad_out[0, 0]
    gain = norm_gain.reshape(1, C)
    low, high = edges(images)
    half = half_time(time_kernel)
    others = round_trip([half] * 3, "y")
    other_half = half_projections(qkv_weight, out_weight, others)
    other_others = round_trip([other_half] * 3, "y")
    rows = conv_forward(images, low, high, incoming, space_kernel)
    tile = exchange(rows)
    times = gathered(four(half, others, half), tile)
    weights = gathered(four(other_half, other_others, rows), tile)
    temporal, normal = temporal_step(tile, gain, times)
    grad_packed, keep, send = attention_step(normal, tile, weights)
    own, *sends = pair_sum(keep, send)
    grad_spatial = exchange(
        tile_gradient(grad_packed, temporal, tile, gain, weights, times, sends[0])
    )
    low, high = edges(grad_spatial)
    grad_latents, token = conv_backward(grad_spatial, low, high, space_kernel)
    grad_qkv, grad_outproj = reduce_grads(own, sends, token)
    return grad_latents[None, None], grad_qkv, grad_outproj


def solution(mesh):
    inner = Mesh(mesh.devices.reshape(2, 4, 4, 2, 4), ("zl", "y", "x", "c", "zh"))
    tiles = P(VIDEO, FRAME, "zh", None, None)
    weight = P(VIDEO, None)
    grads = P(VIDEO, ("x", "c", "zh"))
    return jax.shard_map(
        shards,
        mesh=inner,
        in_specs=(tiles, P(), weight, weight, weight, P(), tiles),
        out_specs=(tiles, grads, grads),
        check_vma=False,
    )
```

```python
import functools

import jax
import jax.numpy as jnp
from jax import lax
from jax.experimental import pallas as pl
from jax.experimental.pallas import tpu as pltpu
from jax.sharding import Mesh
from jax.sharding import PartitionSpec as P

HEAD_DIM = 64
C = 640
F32 = jnp.float32
BF16 = jnp.bfloat16
VIDEO = ("zl", "y")
FRAME = ("x", "c")
MIB = 1 << 20
BLOCKS = (4, 4, 80, C)


def sds(shape, dtype=BF16):
    return jax.ShapeDtypeStruct(shape, dtype)


AXES = ("zl", "y", "x", "c", "zh")


def call(body, outs, n_vmem, n_any, scratch=(), limit=12, flops=0, moved=0):
    def placed_body(*refs):
        body([lax.axis_index(name) for name in AXES], *refs)

    specs = [pl.BlockSpec(memory_space=pltpu.VMEM)] * n_vmem
    specs += [pl.BlockSpec(memory_space=pl.ANY)] * n_any
    return pl.pallas_call(
        placed_body,
        out_shape=outs,
        in_specs=specs,
        out_specs=[pl.BlockSpec(memory_space=pltpu.VMEM)] * len(outs),
        scratch_shapes=list(scratch),
        compiler_params=pltpu.CompilerParams(vmem_limit_bytes=limit * MIB),
        cost_estimate=pl.CostEstimate(flops=flops, bytes_accessed=moved, transcendentals=0),
    )


def mm(a, b):
    return lax.dot_general(a, b, (((1,), (0,)), ((), ())), preferred_element_type=F32)


def mm_nt(a, b):
    return lax.dot_general(a, b, (((1,), (1,)), ((), ())), preferred_element_type=F32)


def mm_tn(a, b):
    return lax.dot_general(a, b, (((0,), (0,)), ((), ())), preferred_element_type=F32)


def shifted_columns(images_ref, low_ref, high_ref, zh, shifts_ref, order):
    low = low_ref[...].astype(F32) * jnp.where(zh > 0, 1.0, 0.0)
    high = high_ref[...].astype(F32) * jnp.where(zh < 3, 1.0, 0.0)
    whole = jnp.concatenate([low, images_ref[...].astype(F32), high], axis=0)
    flat = whole.reshape(320, C)
    column = lax.broadcasted_iota(jnp.int32, (320, C), 0) % 32
    before = jnp.where(column == 0, 0.0, pltpu.roll(flat, 1, 0))
    after = jnp.where(column == 31, 0.0, pltpu.roll(flat, 319, 0))
    views = (before, flat, after)
    for j, which in enumerate(order):
        shifts_ref[:, j * C : (j + 1) * C] = views[which].astype(BF16)


def kernel_copies(kernel_hbm, kernel_ref, sems):
    return [
        pltpu.make_async_copy(kernel_hbm.at[pl.ds(dy, 1)], kernel_ref.at[pl.ds(dy, 1)], sems.at[dy])
        for dy in range(3)
    ]


def conv_forward_body(pos, images, low, high, grad_out, kernel_hbm, out, *rest):
    kernel_ref, shifts, sems = rest
    copies = kernel_copies(kernel_hbm, kernel_ref, sems)
    for copy in copies:
        copy.start()
    shifted_columns(images, low, high, pos[4], shifts, (0, 1, 2))
    total = images[...].astype(F32).reshape(256, C)
    for dy in range(3):
        copies[dy].wait()
        taps = kernel_ref[dy].reshape(3 * C, C)
        total = total + mm(shifts[32 * dy : 32 * dy + 256, :], taps)
    out[:, 0] = total.astype(BF16).reshape(8, 32, C)
    out[:, 1] = grad_out[...]


def conv_backward_body(pos, images, low, high, kernel_hbm, out, token, kernel_ref, shifts, sems):
    token[...] = jnp.zeros((8, 128), F32)
    copies = kernel_copies(kernel_hbm, kernel_ref, sems)
    for copy in copies:
        copy.start()
    shifted_columns(images, low, high, pos[4], shifts, (2, 1, 0))
    total = images[...].astype(F32).reshape(256, C)
    for dy in range(3):
        copies[dy].wait()
        at = 32 * (2 - dy)
        for dx in range(3):
            total = total + mm_nt(shifts[at : at + 256, dx * C : (dx + 1) * C], kernel_ref[dy, dx])
    out[...] = total.astype(BF16).reshape(8, 32, C)


CONV_SCRATCH = (pltpu.VMEM((3, 3, C, C), BF16), pltpu.VMEM((320, 3 * C), BF16))


def conv_forward(images, low, high, grad_out, kernel):
    return call(
        conv_forward_body,
        [sds((8, 2, 32, C))],
        4,
        1,
        CONV_SCRATCH + (pltpu.SemaphoreType.DMA((3,)),),
        limit=48,
        flops=2 * 256 * 9 * C * C,
        moved=9 * C * C * 2,
    )(images, low, high, grad_out, kernel)[0]


def conv_backward(images, low, high, kernel):
    return call(
        conv_backward_body,
        [sds((8, 32, C)), sds((8, 128), F32)],
        3,
        1,
        CONV_SCRATCH + (pltpu.SemaphoreType.DMA((3,)),),
        limit=48,
        flops=2 * 256 * 9 * C * C,
        moved=9 * C * C * 2,
    )(images, low, high, kernel)


def halves_body(pos, time, qkv, out, half, sems):
    core = pos[3]
    rows = time.at[pl.ds(pl.multiple_of(112 * core, 16), 128)]

    def run(first, second):
        copies = [
            pltpu.make_async_copy(rows, half.at[0:128], sems.at[0]),
            pltpu.make_async_copy(first, half.at[128:208], sems.at[1]),
            pltpu.make_async_copy(second, half.at[208:288], sems.at[2]),
        ]
        for copy in copies:
            copy.start()
        for copy in copies:
            copy.wait()

    @pl.when(core == 0)
    def _():
        run(qkv.at[:, 0:C], qkv.at[:, C : 2 * C])

    @pl.when(core == 1)
    def _():
        run(qkv.at[:, 2 * C : 3 * C], out)


def halves_of(time, qkv, out):
    dma = (pltpu.SemaphoreType.DMA((3,)),)
    return call(halves_body, [sds((288, C))], 0, 3, dma, limit=62)(time, qkv, out)[0]


def gate(value, after):
    return pl.pallas_call(
        lambda a, b, c: None,
        out_shape=sds(value.shape, value.dtype),
        in_specs=[pl.BlockSpec(memory_space=pl.ANY)] * 2,
        out_specs=pl.BlockSpec(memory_space=pl.ANY),
        input_output_aliases={0: 0},
    )(value, after)


def four_body(pos, own, *refs):
    others, four, three = refs[:3], refs[-2], refs[-1]
    four[pos[1]] = own[...]
    for k in range(3):
        four[(pos[1] + 3 - k) % 4] = others[k][...]
        three[k] = others[k][...]


def four_of(own, others, *after):
    outs = [sds((4,) + own.shape), sds((3,) + own.shape)]
    return call(four_body, outs, 4, len(after))(own, *others, *after)


def across(own):
    pairs = []
    for z in range(8):
        for core in range(2):
            to = (z + 7 + 2 * core) % 8
            pairs.append(tuple(((at % 2) * 2 + core) * 4 + at // 2 for at in (z, to)))
    return lax.ppermute(own, ("zl", "c", "zh"), pairs)


def swapped(value):
    return lax.ppermute(value, "c", [(0, 1), (1, 0)])


def placed_pieces(pos, pieces):
    zl, y, core = pos[0], pos[1], pos[3]
    own, own_swapped, near, near_swapped, three, three_swapped = pieces
    placed = [(own, pl.ds(4 * zl, 4), core), (own_swapped, pl.ds(4 * zl, 4), 1 - core)]
    for half, one, others in ((core, near, three), (1 - core, near_swapped, three_swapped)):
        placed.append((one, 4 * (1 - zl) + y, half))
        for k in range(3):
            placed.append((others.at[k], 4 * (1 - zl) + (y + 3 - k) % 4, half))
    return placed


def time_copies(pos, pieces, target, sem):
    copies = []
    for i, (piece, blocks, half) in enumerate(placed_pieces(pos, pieces)):
        lead = (slice(None),) if i < 2 else ()

        def part(first, last, n, i=i, piece=piece, blocks=blocks, lead=lead):
            source = piece.at[lead + (pl.ds(pl.multiple_of(first, 16), n),)]
            place = target.at[blocks, pl.ds(pl.multiple_of(last, 16), n)]
            copies.append(pltpu.make_async_copy(source, place, sem.at[len(copies)]))

        part(16 * half, 128 * half, 112)
        if i == 0 or 2 <= i < 6:
            part(112 * (1 - half), 112, 16)
    return copies


def projection_copies(pos, pieces, target, sem):
    copies = []
    for i, (piece, blocks, half) in enumerate(placed_pieces(pos, pieces)):
        lead = (slice(None),) if i < 2 else ()
        for j in range(2):
            lanes = pl.ds(pl.multiple_of(1280 * half + 640 * j, 128), 640)
            source = piece.at[lead + (pl.ds(128 + 80 * j, 80),)]
            place = target.at[blocks, :, lanes]
            copies.append(pltpu.make_async_copy(source, place, sem.at[2 * i + j]))
    return copies


def temporal_body(pos, tile, gain, *refs):
    time_pieces, (temporal_out, normal_out) = refs[:6], refs[6:8]
    time_ref, padded, sem = refs[8:]
    copies = time_copies(pos, time_pieces, time_ref, sem)
    for copy in copies:
        copy.start()
    value = tile[:, 0].astype(F32)
    padded[0] = jnp.zeros((32, C), BF16)
    padded[1:9] = (value * jax.nn.sigmoid(value)).astype(BF16)
    padded[9] = jnp.zeros((32, C), BF16)
    total = value.reshape(256, C)
    for copy in copies:
        copy.wait()
    taps = time_ref[...].reshape(3 * C, C)
    for k in range(3):
        total = total + mm(padded[k : k + 8].reshape(256, C), taps[k * C : (k + 1) * C, :])
    temporal = total.astype(BF16)
    temporal_out[...] = temporal
    value = temporal.astype(F32)
    scale = lax.rsqrt(jnp.mean(value * value, axis=-1, keepdims=True) + 1e-06)
    normal_out[...] = (value * scale * gain[...]).astype(BF16)


TIME_SCRATCH = (pltpu.VMEM((8, 240, C), BF16), pltpu.VMEM((10, 32, C), BF16))


def temporal_step(tile, gain, time_pieces):
    return call(
        temporal_body,
        [sds((256, C)), sds((256, C))],
        2,
        6,
        TIME_SCRATCH + (pltpu.SemaphoreType.DMA((15,)),),
        limit=20,
        flops=2 * 256 * 3 * C * C,
        moved=3 * C * C * 2,
    )(tile, gain, *time_pieces)


def attention_body(pos, normal, tile, *refs):
    weight_pieces, (grad_packed, mixed_out, send) = refs[:6], refs[6:9]
    weight_ref, packed, grad_blend, blended, sem = refs[9:]
    copies = projection_copies(pos, weight_pieces, weight_ref, sem)
    for copy in copies:
        copy.start()
    for copy in copies:
        copy.wait()
    weight = weight_ref[...].reshape(C, 4 * C)
    packed[...] = mm(normal[...], weight[:, : 3 * C]).astype(BF16).reshape(8, 2, 16, 3 * C)
    grad_blend[...] = mm_nt(tile[:, 1].reshape(256, C), weight[:, 3 * C :]).astype(BF16).reshape(8, 2, 16, C)
    first_head = lax.broadcasted_iota(jnp.int32, (128, 128), 1) < HEAD_DIM
    row_pixel = lax.broadcasted_iota(jnp.int32, (256, 128), 0) % 16
    column_pixel = lax.broadcasted_iota(jnp.int32, (256, 128), 1) % 16
    same_pixel = row_pixel == column_pixel
    nothing = jnp.zeros((128, 128), BF16)

    def two_heads(block):
        return jnp.concatenate(
            [jnp.where(first_head, block, nothing), jnp.where(first_head, nothing, block)], axis=0
        )

    def merged(both):
        return jnp.where(first_head, both[:128], both[128:]).astype(BF16)

    for half in range(2):
        for pair in range(5):
            at = pair * 128

            def part(ref, offset):
                return ref[:, half, :, offset + at : offset + at + 128].reshape(128, 128)

            queries = two_heads(part(packed, 0))
            keys = part(packed, C)
            values = part(packed, 2 * C)
            scores = jnp.where(same_pixel, mm_nt(queries, keys) * HEAD_DIM**-0.5, -1e30)
            expons = jnp.exp(scores - jnp.max(scores, axis=-1, keepdims=True))
            probs = expons * (1.0 / jnp.sum(expons, axis=-1, keepdims=True))
            rounded = probs.astype(BF16)
            blended[:, half, :, at : at + 128] = merged(mm(rounded, values)).reshape(8, 16, 128)
            upper = two_heads(part(grad_blend, 0))
            grad_probs = mm_nt(upper, values)
            inner = jnp.sum(grad_probs * probs, axis=-1, keepdims=True)
            grad_scores = (probs * (grad_probs - inner) * HEAD_DIM**-0.5).astype(BF16)
            results = (
                merged(mm(grad_scores, keys)),
                mm_tn(grad_scores, queries).astype(BF16),
                mm_tn(rounded, upper).astype(BF16),
            )
            for i, result in enumerate(results):
                lanes = slice(i * C + at, i * C + at + 128)
                grad_packed[:, half, :, lanes] = result.reshape(8, 16, 128)

    mixed_out[...] = blended[...].reshape(256, C)
    weight_gradient(1 - pos[3], normal, mixed_out, tile, grad_packed, send)


def gradient_pair(first, second):
    def gap(n):
        return jnp.zeros((256, n), BF16)

    def placed(left, *parts):
        return mm_tn(left, jnp.concatenate(parts, axis=1))

    a = placed(first[0], first[2], gap(16))
    b = placed(first[1], gap(112), first[3], gap(64))
    c = placed(second[0], gap(64), second[2], gap(80))
    d = placed(second[1], gap(48), second[3])
    groups = (
        a[:, :128],
        a[:, 128:] + b[:, :128],
        b[:, 128:] + c[:, :128],
        c[:, 128:256],
        c[:, 256:] + d,
    )
    return jnp.concatenate(groups, axis=1).astype(BF16)


def weight_gradient(core, normal, mixed, tile, grad_packed, target):
    for which in range(2):

        @pl.when(core == which)
        def _(which=which):
            packed = grad_packed[...].reshape(256, 3 * C)
            arriving = tile[:, 1].reshape(256, C)
            left, right = normal[...], mixed[...]

            def sides(x):
                at = 2 * x + which
                return packed[:, 240 * at : 240 * at + 240], arriving[:, 80 * at : 80 * at + 80]

            if which == 0:
                for half in range(2):
                    a, b = [(left, right) + sides(2 * half + i) for i in range(2)]
                    both = gradient_pair(a, b).reshape(2, 4, 80, C)
                    for zl in range(2):
                        target[:, 2 * zl + half] = both[zl]
            else:
                lefts = left[:, :320], left[:, 320:]
                rights = right[:, :320], right[:, 320:]
                for x in range(4):
                    a, b = [(lefts[zl], rights[zl]) + sides(x) for zl in range(2)]
                    target[x] = gradient_pair(a, b).reshape(4, 80, C)


def own_gradient_body(pos, normal, mixed, tile, grad_packed, keep):
    weight_gradient(pos[3], normal, mixed, tile, grad_packed, keep)


def own_gradient(normal, mixed, tile, grad_packed):
    return call(
        own_gradient_body,
        [sds(BLOCKS)],
        4,
        0,
        limit=24,
        flops=2 * 256 * 2 * C * C,
        moved=2 * C * C * 2,
    )(normal, mixed, tile, grad_packed)[0]


def attention_step(normal, tile, weight_pieces):
    return call(
        attention_body,
        [sds((8, 2, 16, 3 * C)), sds((256, C)), sds(BLOCKS)],
        2,
        6,
        (
            pltpu.VMEM((8, 80, 4 * C), BF16),
            pltpu.VMEM((8, 2, 16, 3 * C), BF16),
            pltpu.VMEM((8, 2, 16, C), BF16),
            pltpu.VMEM((8, 2, 16, C), BF16),
            pltpu.SemaphoreType.DMA((20,)),
        ),
        limit=36,
        flops=2 * 256 * 8 * C * C,
        moved=4 * C * C * 2,
    )(normal, tile, *weight_pieces)


def tile_gradient_body(pos, *refs):
    grad_packed, temporal, tile, gain = refs[:4]
    pieces, out = refs[4:10], refs[11]
    weight_ref, time_ref, padded, sem, time_sem = refs[12:]
    copies = projection_copies(pos, pieces, weight_ref, sem)
    later_copies = time_copies(pos, pieces, time_ref, time_sem)
    for copy in copies + later_copies:
        copy.start()
    for copy in copies:
        copy.wait()
    weight = weight_ref[...].reshape(C, 4 * C)[:, : 3 * C]
    grad_normal = mm_nt(grad_packed[...].reshape(256, 3 * C), weight)
    value = temporal[...].astype(F32)
    scale = lax.rsqrt(jnp.mean(value * value, axis=-1, keepdims=True) + 1e-06)
    scaled = grad_normal * gain[...]
    inner = jnp.mean(value * scaled, axis=-1, keepdims=True)
    through_norm = scale * scaled - value * (scale * scale * scale * inner)
    grad_temporal = (tile[:, 1].astype(F32).reshape(256, C) + through_norm).astype(BF16)
    padded[0] = jnp.zeros((32, C), BF16)
    padded[1:9] = grad_temporal.reshape(8, 32, C)
    padded[9] = jnp.zeros((32, C), BF16)
    for copy in later_copies:
        copy.wait()
    taps = time_ref[...].reshape(3 * C, C)
    grad_act = jnp.zeros((256, C), F32)
    for k in range(3):
        later = padded[2 - k : 10 - k].reshape(256, C)
        grad_act = grad_act + mm_nt(later, taps[k * C : (k + 1) * C, :])
    as_float = tile[:, 0].astype(F32).reshape(256, C)
    logistic = jax.nn.sigmoid(as_float)
    grad_spatial = grad_temporal.astype(F32) + grad_act * logistic * (
        1.0 + as_float * (1.0 - logistic)
    )
    out[...] = grad_spatial.astype(BF16).reshape(8, 32, C)


def tile_gradient(grad_packed, temporal, tile, gain, weights, after):
    return call(
        tile_gradient_body,
        [sds((8, 32, C))],
        4,
        7,
        (pltpu.VMEM((8, 80, 4 * C), BF16),)
        + TIME_SCRATCH
        + (pltpu.SemaphoreType.DMA((20,)), pltpu.SemaphoreType.DMA((15,))),
        limit=28,
        flops=2 * 256 * 6 * C * C,
        moved=7 * C * C * 2,
    )(grad_packed, temporal, tile, gain, *weights, after)[0]


def pair_sum_body(pos, keep, other, own, *sends):
    me = jnp.where(pos[3] == 0, pos[1], pos[2])

    def block(index):
        return keep[index].astype(F32) + other[index].astype(F32)

    own[...] = block(me)
    for k in range(3):
        sends[k][...] = block((me + k + 1) % 4).astype(BF16)


def second_sum_body(pos, held, *refs):
    others, own, sends, scratch = refs[0:3], refs[3], refs[4:7], refs[7]
    total = held[...]
    for other in others:
        total = total + other[...].astype(F32)

    for which in range(2):

        @pl.when(pos[3] == which)
        def _(which=which):
            for i in range(4):
                for zl in range(2):
                    block, at = (2 * zl + i // 2, i % 2) if which == 0 else (i, zl)
                    scratch[i, zl] = total[block, :, 320 * at : 320 * at + 320]

    me = jnp.where(pos[3] == 0, pos[2], pos[1])
    own[...] = scratch[me]
    for k in range(3):
        sends[k][...] = scratch[(me + k + 1) % 4].astype(BF16)


def third_sum_body(pos, held, first, second, third, out):
    total = held[...]
    for other in (first, second, third):
        total = total + other[...].astype(F32)
    for row in range(4):
        out[row, :, :, 0:60] = total[:, :, 60 * row : 60 * row + 60].astype(BF16)
        out[row, :, :, 60:80] = total[:, :, 240 + 20 * row : 240 + 20 * row + 20].astype(BF16)


def row_sum_body(pos, parts, after, own, send, scratch):
    scratch[...] = jnp.sum(parts[...].astype(F32), axis=0)
    own[...] = scratch[pos[0]]
    send[...] = scratch[1 - pos[0]].astype(BF16)


def last_sum_body(pos, held, other, qkv_out, out_out):
    total = (held[...] + other[...].astype(F32)).T
    qkv_out[...] = total[0:60]
    out_out[...] = total[60:80]


def round_trip(sends, axis):
    return [
        lax.ppermute(sends[k], axis, [(i, (i + k + 1) % 4) for i in range(4)]) for k in range(3)
    ]


def crosswise(sends, first):
    def target(y, x, core, k):
        if (core == 0) == first:
            return (y + k + 1) % 4, x
        return y, (x + k + 1) % 4

    moved = []
    for k in range(3):
        pairs = []
        for y in range(4):
            for x in range(4):
                for core in range(2):
                    ty, tx = target(y, x, core, k)
                    pairs.append(((y * 4 + x) * 2 + core, (ty * 4 + tx) * 2 + core))
        moved.append(lax.ppermute(sends[k], ("y", "x", "c"), pairs))
    return moved


def pair_sum(keep, send):
    step = BLOCKS[1:]
    return call(pair_sum_body, [sds(step, F32)] + [sds(step)] * 3, 2, 0, limit=20)(
        keep, swapped(send)
    )


def reduce_grads(summed, after):
    own, *sends = summed
    step = (2, 80, 320)
    own, *sends = call(
        second_sum_body,
        [sds(step, F32)] + [sds(step)] * 3,
        4,
        0,
        (pltpu.VMEM((4,) + step, F32),),
        limit=20,
    )(own, *crosswise(sends, True))
    parts = call(third_sum_body, [sds((4, 2, 80, 80))], 4, 0)(own, *crosswise(sends, False))[0]
    parts = lax.all_to_all(parts, "zh", split_axis=0, concat_axis=0, tiled=True)
    own, send = call(
        row_sum_body, [sds((80, 80), F32), sds((80, 80))], 1, 1, (pltpu.VMEM((2, 80, 80), F32),)
    )(parts, after)
    other = lax.ppermute(send, "zl", [(0, 1), (1, 0)])
    grads = call(last_sum_body, [sds((60, 80), F32), sds((20, 80), F32)], 2, 0)(own, other)
    return [grad.T for grad in grads]


def edges(images):
    low = lax.ppermute(images[7:8], "zh", [(i, (i + 1) % 4) for i in range(4)])
    high = lax.ppermute(images[0:1], "zh", [(i, (i + 3) % 4) for i in range(4)])
    return low, high


def exchange(rows):
    return lax.all_to_all(rows, FRAME, split_axis=0, concat_axis=0, tiled=True)


def shards(latents, space_kernel, time_kernel, qkv_weight, out_weight, norm_gain, grad_out):
    images, incoming = latents[0, 0], grad_out[0, 0]
    gain = norm_gain.reshape(1, C)
    low, high = edges(images)
    half = halves_of(time_kernel, qkv_weight, out_weight)
    others = round_trip([half] * 3, "y")
    near = across(half)
    rows = conv_forward(images, low, high, incoming, space_kernel)
    tile = exchange(rows)
    own, three = four_of(half, others, rows, near)
    far = gate(across(three), tile)
    weights = [own, swapped(own), near, swapped(near), far, swapped(far)]
    temporal, normal = temporal_step(tile, gain, weights)
    grad_packed, mixed, send = attention_step(normal, tile, weights)
    keep = own_gradient(normal, mixed, tile, grad_packed)
    summed = pair_sum(keep, send)
    grad_spatial = exchange(
        tile_gradient(grad_packed, temporal, tile, gain, weights, summed[0])
    )
    low, high = edges(grad_spatial)
    grad_latents, token = conv_backward(grad_spatial, low, high, space_kernel)
    grad_qkv, grad_outproj = reduce_grads(summed, token)
    return grad_latents[None, None], grad_qkv, grad_outproj


def solution(mesh):
    inner = Mesh(mesh.devices.reshape(2, 4, 4, 2, 4), ("zl", "y", "x", "c", "zh"))
    tiles = P(VIDEO, FRAME, "zh", None, None)
    weight = P(VIDEO, None)
    grads = P(VIDEO, ("x", "c", "zh"))
    return jax.shard_map(
        shards,
        mesh=inner,
        in_specs=(tiles, P(), weight, weight, weight, P(), tiles),
        out_specs=(tiles, grads, grads),
        check_vma=False,
    )
```

```python
import functools

import jax
import jax.numpy as jnp
from jax import lax
from jax.experimental import pallas as pl
from jax.experimental.pallas import tpu as pltpu
from jax.sharding import Mesh
from jax.sharding import PartitionSpec as P

HEAD_DIM = 64
C = 640
F32 = jnp.float32
BF16 = jnp.bfloat16
VIDEO = ("zl", "y")
FRAME = ("x", "c")
MIB = 1 << 20
BLOCKS = (4, 4, 80, C)


def sds(shape, dtype=BF16):
    return jax.ShapeDtypeStruct(shape, dtype)


AXES = ("zl", "y", "x", "c", "zh")


def call(body, outs, n_vmem, n_any, scratch=(), limit=12, flops=0, moved=0):
    def placed_body(*refs):
        body([lax.axis_index(name) for name in AXES], *refs)

    specs = [pl.BlockSpec(memory_space=pltpu.VMEM)] * n_vmem
    specs += [pl.BlockSpec(memory_space=pl.ANY)] * n_any
    return pl.pallas_call(
        placed_body,
        out_shape=outs,
        in_specs=specs,
        out_specs=[pl.BlockSpec(memory_space=pltpu.VMEM)] * len(outs),
        scratch_shapes=list(scratch),
        compiler_params=pltpu.CompilerParams(vmem_limit_bytes=limit * MIB),
        cost_estimate=pl.CostEstimate(flops=flops, bytes_accessed=moved, transcendentals=0),
    )


def mm(a, b):
    return lax.dot_general(a, b, (((1,), (0,)), ((), ())), preferred_element_type=F32)


def mm_nt(a, b):
    return lax.dot_general(a, b, (((1,), (1,)), ((), ())), preferred_element_type=F32)


def mm_tn(a, b):
    return lax.dot_general(a, b, (((0,), (0,)), ((), ())), preferred_element_type=F32)


def shifted_columns(images_ref, low_ref, high_ref, zh, shifts_ref, order):
    low = low_ref[...].astype(F32) * jnp.where(zh > 0, 1.0, 0.0)
    high = high_ref[...].astype(F32) * jnp.where(zh < 3, 1.0, 0.0)
    whole = jnp.concatenate([low, images_ref[...].astype(F32), high], axis=0)
    flat = whole.reshape(320, C)
    column = lax.broadcasted_iota(jnp.int32, (320, C), 0) % 32
    before = jnp.where(column == 0, 0.0, pltpu.roll(flat, 1, 0))
    after = jnp.where(column == 31, 0.0, pltpu.roll(flat, 319, 0))
    views = (before, flat, after)
    for j, which in enumerate(order):
        shifts_ref[:, j * C : (j + 1) * C] = views[which].astype(BF16)


def kernel_copies(kernel_hbm, kernel_ref, sems):
    copies = []
    for dx in range(3):
        tap = (pl.ds(0, 1), pl.ds(dx, 1))
        copies.append(pltpu.make_async_copy(kernel_hbm.at[tap], kernel_ref.at[tap], sems.at[dx]))
    for dy in (1, 2):
        row = (pl.ds(dy, 1),)
        copies.append(pltpu.make_async_copy(kernel_hbm.at[row], kernel_ref.at[row], sems.at[dy + 2]))
    return copies


def conv_forward_body(pos, low, high, images_hbm, grad_hbm, kernel_hbm, out, *scratch):
    kernel_ref, shifts, sems, images, image_sems = scratch
    inputs = [
        pltpu.make_async_copy(images_hbm, images, image_sems.at[0]),
        pltpu.make_async_copy(grad_hbm, out.at[:, 1], image_sems.at[1]),
    ]
    copies = kernel_copies(kernel_hbm, kernel_ref, sems)
    for copy in inputs[:1] + copies + inputs[1:]:
        copy.start()
    inputs[0].wait()
    shifted_columns(images, low, high, pos[4], shifts, (0, 1, 2))
    total = images[...].astype(F32).reshape(256, C)
    for dx in range(3):
        copies[dx].wait()
        total = total + mm(shifts[0:256, dx * C : (dx + 1) * C], kernel_ref[0, dx])
    for dy in (1, 2):
        copies[dy + 2].wait()
        taps = kernel_ref[dy].reshape(3 * C, C)
        total = total + mm(shifts[32 * dy : 32 * dy + 256, :], taps)
    out[:, 0] = total.astype(BF16).reshape(8, 32, C)
    inputs[1].wait()


def conv_backward_body(pos, images, low, high, kernel_hbm, out, token, kernel_ref, shifts, sems):
    token[...] = jnp.zeros((8, 128), F32)
    copies = kernel_copies(kernel_hbm, kernel_ref, sems)
    for copy in copies:
        copy.start()
    shifted_columns(images, low, high, pos[4], shifts, (2, 1, 0))
    total = images[...].astype(F32).reshape(256, C)
    for dy in range(3):
        at = 32 * (2 - dy)
        if dy > 0:
            copies[dy + 2].wait()
        for dx in range(3):
            if dy == 0:
                copies[dx].wait()
            total = total + mm_nt(shifts[at : at + 256, dx * C : (dx + 1) * C], kernel_ref[dy, dx])
    out[...] = total.astype(BF16).reshape(8, 32, C)


CONV_SCRATCH = (pltpu.VMEM((3, 3, C, C), BF16), pltpu.VMEM((320, 3 * C), BF16))


def conv_forward(images, low, high, grad_out, kernel):
    return call(
        conv_forward_body,
        [sds((8, 2, 32, C))],
        2,
        3,
        CONV_SCRATCH
        + (
            pltpu.SemaphoreType.DMA((5,)),
            pltpu.VMEM((8, 32, C), BF16),
            pltpu.SemaphoreType.DMA((2,)),
        ),
        limit=48,
        flops=2 * 256 * 9 * C * C,
        moved=9 * C * C * 2,
    )(low, high, images, grad_out, kernel)[0]


def conv_backward(images, low, high, kernel):
    return call(
        conv_backward_body,
        [sds((8, 32, C)), sds((8, 128), F32)],
        3,
        1,
        CONV_SCRATCH + (pltpu.SemaphoreType.DMA((5,)),),
        limit=48,
        flops=2 * 256 * 9 * C * C,
        moved=9 * C * C * 2,
    )(images, low, high, kernel)


def halves_body(pos, time, qkv, out, images, half, twin, top, bottom, sems):
    core = pos[3]
    rows = time.at[pl.ds(pl.multiple_of(112 * core, 16), 128)]

    def run(first, second):
        moves = [(images.at[pl.ds(0, 1)], top), (images.at[pl.ds(7, 1)], bottom)]
        for target in (half, twin):
            moves.append((rows, target.at[0:128]))
            moves.append((first, target.at[128:208]))
            moves.append((second, target.at[208:288]))
        copies = [pltpu.make_async_copy(a, b, sems.at[i]) for i, (a, b) in enumerate(moves)]
        for copy in copies:
            copy.start()
        for copy in copies:
            copy.wait()

    @pl.when(core == 0)
    def _():
        run(qkv.at[:, 0:C], qkv.at[:, C : 2 * C])

    @pl.when(core == 1)
    def _():
        run(qkv.at[:, 2 * C : 3 * C], out)


def halves_of(time, qkv, out, images):
    dma = (pltpu.SemaphoreType.DMA((8,)),)
    outs = [sds((288, C))] * 2 + [sds((1, 32, C))] * 2
    return call(halves_body, outs, 0, 4, dma, limit=62)(time, qkv, out, images)


def gate(value, after):
    return pl.pallas_call(
        lambda a, b, c: None,
        out_shape=sds(value.shape, value.dtype),
        in_specs=[pl.BlockSpec(memory_space=pl.ANY)] * 2,
        out_specs=pl.BlockSpec(memory_space=pl.ANY),
        input_output_aliases={0: 0},
        compiler_params=pltpu.CompilerParams(vmem_limit_bytes=MIB),
    )(value, after)


def four_body(pos, own, *refs):
    others, four, three = refs[:3], refs[-2], refs[-1]
    four[pos[1]] = own[...]
    for k in range(3):
        four[(pos[1] + 3 - k) % 4] = others[k][...]
        three[k] = others[k][...]


def four_of(own, others, *after):
    outs = [sds((4,) + own.shape), sds((3,) + own.shape)]
    return call(four_body, outs, 4, len(after))(own, *others, *after)


def across(own):
    pairs = []
    for z in range(8):
        for core in range(2):
            to = (z + 7 + 2 * core) % 8
            pairs.append(tuple(((at % 2) * 2 + core) * 4 + at // 2 for at in (z, to)))
    return lax.ppermute(own, ("zl", "c", "zh"), pairs)


def swapped(value):
    return lax.ppermute(value, "c", [(0, 1), (1, 0)])


def placed_pieces(pos, pieces):
    zl, y, core = pos[0], pos[1], pos[3]
    own, own_swapped, near, near_swapped, three, three_swapped = pieces
    placed = [(own, pl.ds(4 * zl, 4), core), (own_swapped, pl.ds(4 * zl, 4), 1 - core)]
    for half, one, others in ((core, near, three), (1 - core, near_swapped, three_swapped)):
        placed.append((one, 4 * (1 - zl) + y, half))
        for k in range(3):
            placed.append((others.at[k], 4 * (1 - zl) + (y + 3 - k) % 4, half))
    return placed


def time_copies(pos, pieces, target, sem):
    copies = []
    for i, (piece, blocks, half) in enumerate(placed_pieces(pos, pieces)):
        lead = (slice(None),) if i < 2 else ()

        def part(first, last, n, i=i, piece=piece, blocks=blocks, lead=lead):
            source = piece.at[lead + (pl.ds(pl.multiple_of(first, 16), n),)]
            place = target.at[blocks, pl.ds(pl.multiple_of(last, 16), n)]
            copies.append(pltpu.make_async_copy(source, place, sem.at[len(copies)]))

        part(16 * half, 128 * half, 112)
        if i == 0 or 2 <= i < 6:
            part(112 * (1 - half), 112, 16)
    return copies


def projection_copies(pos, pieces, target, sem):
    copies = []
    for i, (piece, blocks, half) in enumerate(placed_pieces(pos, pieces)):
        lead = (slice(None),) if i < 2 else ()
        for j in range(2):
            lanes = pl.ds(pl.multiple_of(1280 * half + 640 * j, 128), 640)
            source = piece.at[lead + (pl.ds(128 + 80 * j, 80),)]
            place = target.at[blocks, :, lanes]
            copies.append(pltpu.make_async_copy(source, place, sem.at[2 * i + j]))
    return copies


def temporal_body(pos, tile, gain, *refs):
    pieces, (temporal_out, normal_out, time_ref, weight_ref) = refs[:6], refs[6:10]
    padded, sem, weight_sem = refs[10:]
    copies = time_copies(pos, pieces, time_ref, sem)
    later_copies = projection_copies(pos, pieces, weight_ref, weight_sem)
    for copy in copies + later_copies:
        copy.start()
    value = tile[:, 0].astype(F32)
    padded[0] = jnp.zeros((32, C), BF16)
    padded[1:9] = (value * jax.nn.sigmoid(value)).astype(BF16)
    padded[9] = jnp.zeros((32, C), BF16)
    total = value.reshape(256, C)
    for copy in copies:
        copy.wait()
    taps = time_ref[...].reshape(3 * C, C)
    for k in range(3):
        total = total + mm(padded[k : k + 8].reshape(256, C), taps[k * C : (k + 1) * C, :])
    temporal = total.astype(BF16)
    temporal_out[...] = temporal
    value = temporal.astype(F32)
    scale = lax.rsqrt(jnp.mean(value * value, axis=-1, keepdims=True) + 1e-06)
    normal_out[...] = (value * scale * gain[...]).astype(BF16)
    for copy in later_copies:
        copy.wait()


PADDED = (pltpu.VMEM((10, 32, C), BF16),)


def temporal_step(tile, gain, pieces):
    return call(
        temporal_body,
        [sds((256, C)), sds((256, C)), sds((8, 240, C)), sds((8, 80, 4 * C))],
        2,
        6,
        PADDED + (pltpu.SemaphoreType.DMA((15,)), pltpu.SemaphoreType.DMA((20,))),
        limit=24,
        flops=2 * 256 * 3 * C * C,
        moved=3 * C * C * 2,
    )(tile, gain, *pieces)


def attention_body(pos, normal, tile, weight_ref, grad_packed, mixed_out, send, *scratch):
    packed, grad_blend, blended = scratch
    weight = weight_ref[...].reshape(C, 4 * C)
    packed[...] = mm(normal[...], weight[:, : 3 * C]).astype(BF16).reshape(8, 2, 16, 3 * C)
    grad_blend[...] = mm_nt(tile[:, 1].reshape(256, C), weight[:, 3 * C :]).astype(BF16).reshape(8, 2, 16, C)
    first_head = lax.broadcasted_iota(jnp.int32, (128, 128), 1) < HEAD_DIM
    row_pixel = lax.broadcasted_iota(jnp.int32, (256, 128), 0) % 16
    column_pixel = lax.broadcasted_iota(jnp.int32, (256, 128), 1) % 16
    same_pixel = row_pixel == column_pixel
    nothing = jnp.zeros((128, 128), BF16)

    def two_heads(block):
        return jnp.concatenate(
            [jnp.where(first_head, block, nothing), jnp.where(first_head, nothing, block)], axis=0
        )

    def merged(both):
        return jnp.where(first_head, both[:128], both[128:]).astype(BF16)

    for half in range(2):
        for pair in range(5):
            at = pair * 128

            def part(ref, offset):
                return ref[:, half, :, offset + at : offset + at + 128].reshape(128, 128)

            queries = two_heads(part(packed, 0))
            keys = part(packed, C)
            values = part(packed, 2 * C)
            scores = jnp.where(same_pixel, mm_nt(queries, keys) * HEAD_DIM**-0.5, -1e30)
            expons = jnp.exp(scores - jnp.max(scores, axis=-1, keepdims=True))
            probs = expons * (1.0 / jnp.sum(expons, axis=-1, keepdims=True))
            rounded = probs.astype(BF16)
            blended[:, half, :, at : at + 128] = merged(mm(rounded, values)).reshape(8, 16, 128)
            upper = two_heads(part(grad_blend, 0))
            grad_probs = mm_nt(upper, values)
            inner = jnp.sum(grad_probs * probs, axis=-1, keepdims=True)
            grad_scores = (probs * (grad_probs - inner) * HEAD_DIM**-0.5).astype(BF16)
            results = (
                merged(mm(grad_scores, keys)),
                mm_tn(grad_scores, queries).astype(BF16),
                mm_tn(rounded, upper).astype(BF16),
            )
            for i, result in enumerate(results):
                lanes = slice(i * C + at, i * C + at + 128)
                grad_packed[:, half, :, lanes] = result.reshape(8, 16, 128)

    mixed_out[...] = blended[...].reshape(256, C)
    weight_gradient(1 - pos[3], normal, mixed_out, tile, grad_packed, send)


def gradient_pair(first, second):
    def gap(n):
        return jnp.zeros((256, n), BF16)

    def placed(left, *parts):
        return mm_tn(left, jnp.concatenate(parts, axis=1))

    a = placed(first[0], first[2], gap(16))
    b = placed(first[1], gap(112), first[3], gap(64))
    c = placed(second[0], gap(64), second[2], gap(80))
    d = placed(second[1], gap(48), second[3])
    groups = (
        a[:, :128],
        a[:, 128:] + b[:, :128],
        b[:, 128:] + c[:, :128],
        c[:, 128:256],
        c[:, 256:] + d,
    )
    return jnp.concatenate(groups, axis=1).astype(BF16)


def weight_gradient(core, normal, mixed, tile, grad_packed, target):
    for which in range(2):

        @pl.when(core == which)
        def _(which=which):
            packed = grad_packed[...].reshape(256, 3 * C)
            arriving = tile[:, 1].reshape(256, C)
            left, right = normal[...], mixed[...]

            def sides(x):
                at = 2 * x + which
                return packed[:, 240 * at : 240 * at + 240], arriving[:, 80 * at : 80 * at + 80]

            if which == 0:
                for half in range(2):
                    a, b = [(left, right) + sides(2 * half + i) for i in range(2)]
                    both = gradient_pair(a, b).reshape(2, 4, 80, C)
                    for zl in range(2):
                        target[:, 2 * zl + half] = both[zl]
            else:
                lefts = left[:, :320], left[:, 320:]
                rights = right[:, :320], right[:, 320:]
                for x in range(4):
                    a, b = [(lefts[zl], rights[zl]) + sides(x) for zl in range(2)]
                    target[x] = gradient_pair(a, b).reshape(4, 80, C)


def own_gradient_body(pos, normal, mixed, tile, grad_packed, keep):
    weight_gradient(pos[3], normal, mixed, tile, grad_packed, keep)


def own_gradient(normal, mixed, tile, grad_packed):
    return call(
        own_gradient_body,
        [sds(BLOCKS)],
        4,
        0,
        limit=24,
        flops=2 * 256 * 2 * C * C,
        moved=2 * C * C * 2,
    )(normal, mixed, tile, grad_packed)[0]


def attention_step(normal, tile, weight):
    return call(
        attention_body,
        [sds((8, 2, 16, 3 * C)), sds((256, C)), sds(BLOCKS)],
        3,
        0,
        (
            pltpu.VMEM((8, 2, 16, 3 * C), BF16),
            pltpu.VMEM((8, 2, 16, C), BF16),
            pltpu.VMEM((8, 2, 16, C), BF16),
        ),
        limit=32,
        flops=2 * 256 * 8 * C * C,
        moved=4 * C * C * 2,
    )(normal, tile, weight)


def tile_gradient_body(pos, *refs):
    grad_packed, temporal, tile, gain, weight_ref, time_ref, _, out, padded = refs
    weight = weight_ref[...].reshape(C, 4 * C)[:, : 3 * C]
    grad_normal = mm_nt(grad_packed[...].reshape(256, 3 * C), weight)
    value = temporal[...].astype(F32)
    scale = lax.rsqrt(jnp.mean(value * value, axis=-1, keepdims=True) + 1e-06)
    scaled = grad_normal * gain[...]
    inner = jnp.mean(value * scaled, axis=-1, keepdims=True)
    through_norm = scale * scaled - value * (scale * scale * scale * inner)
    grad_temporal = (tile[:, 1].astype(F32).reshape(256, C) + through_norm).astype(BF16)
    padded[0] = jnp.zeros((32, C), BF16)
    padded[1:9] = grad_temporal.reshape(8, 32, C)
    padded[9] = jnp.zeros((32, C), BF16)
    taps = time_ref[...].reshape(3 * C, C)
    grad_act = jnp.zeros((256, C), F32)
    for k in range(3):
        later = padded[2 - k : 10 - k].reshape(256, C)
        grad_act = grad_act + mm_nt(later, taps[k * C : (k + 1) * C, :])
    as_float = tile[:, 0].astype(F32).reshape(256, C)
    logistic = jax.nn.sigmoid(as_float)
    grad_spatial = grad_temporal.astype(F32) + grad_act * logistic * (
        1.0 + as_float * (1.0 - logistic)
    )
    out[...] = grad_spatial.astype(BF16).reshape(8, 32, C)


def tile_gradient(grad_packed, temporal, tile, gain, weight, time, after):
    return call(
        tile_gradient_body,
        [sds((8, 32, C))],
        6,
        1,
        PADDED,
        limit=24,
        flops=2 * 256 * 6 * C * C,
        moved=7 * C * C * 2,
    )(grad_packed, temporal, tile, gain, weight, time, after)[0]


def pair_sum_body(pos, keep, other, own, *sends):
    me = jnp.where(pos[3] == 0, pos[1], pos[2])

    def block(index):
        return keep[index].astype(F32) + other[index].astype(F32)

    own[...] = block(me)
    for k in range(3):
        sends[k][...] = block((me + k + 1) % 4).astype(BF16)


def second_sum_body(pos, held, *refs):
    others, own, sends, scratch = refs[0:3], refs[3], refs[4:7], refs[7]
    total = held[...]
    for other in others:
        total = total + other[...].astype(F32)

    for which in range(2):

        @pl.when(pos[3] == which)
        def _(which=which):
            for i in range(4):
                for zl in range(2):
                    block, at = (2 * zl + i // 2, i % 2) if which == 0 else (i, zl)
                    scratch[i, zl] = total[block, :, 320 * at : 320 * at + 320]

    me = jnp.where(pos[3] == 0, pos[2], pos[1])
    own[...] = scratch[me]
    for k in range(3):
        sends[k][...] = scratch[(me + k + 1) % 4].astype(BF16)


def third_sum_body(pos, held, first, second, third, out):
    total = held[...]
    for other in (first, second, third):
        total = total + other[...].astype(F32)
    for row in range(4):
        out[row, :, :, 0:60] = total[:, :, 60 * row : 60 * row + 60].astype(BF16)
        out[row, :, :, 60:80] = total[:, :, 240 + 20 * row : 240 + 20 * row + 20].astype(BF16)


def row_sum_body(pos, parts, after, own, send, scratch):
    scratch[...] = jnp.sum(parts[...].astype(F32), axis=0)
    own[...] = scratch[pos[0]]
    send[...] = scratch[1 - pos[0]].astype(BF16)


def last_sum_body(pos, held, other, qkv_out, out_out):
    total = (held[...] + other[...].astype(F32)).T
    qkv_out[...] = total[0:60]
    out_out[...] = total[60:80]


def round_trip(sends, axis):
    return [
        lax.ppermute(sends[k], axis, [(i, (i + k + 1) % 4) for i in range(4)]) for k in range(3)
    ]


def crosswise(sends, first):
    def target(y, x, core, k):
        if (core == 0) == first:
            return (y + k + 1) % 4, x
        return y, (x + k + 1) % 4

    moved = []
    for k in range(3):
        pairs = []
        for y in range(4):
            for x in range(4):
                for core in range(2):
                    ty, tx = target(y, x, core, k)
                    pairs.append(((y * 4 + x) * 2 + core, (ty * 4 + tx) * 2 + core))
        moved.append(lax.ppermute(sends[k], ("y", "x", "c"), pairs))
    return moved


def pair_sum(keep, send):
    step = BLOCKS[1:]
    return call(pair_sum_body, [sds(step, F32)] + [sds(step)] * 3, 2, 0, limit=20)(
        keep, swapped(send)
    )


def reduce_grads(summed, after):
    own, *sends = summed
    step = (2, 80, 320)
    own, *sends = call(
        second_sum_body,
        [sds(step, F32)] + [sds(step)] * 3,
        4,
        0,
        (pltpu.VMEM((4,) + step, F32),),
        limit=20,
    )(own, *crosswise(sends, True))
    parts = call(third_sum_body, [sds((4, 2, 80, 80))], 4, 0)(own, *crosswise(sends, False))[0]
    parts = lax.all_to_all(parts, "zh", split_axis=0, concat_axis=0, tiled=True)
    own, send = call(
        row_sum_body, [sds((80, 80), F32), sds((80, 80))], 1, 1, (pltpu.VMEM((2, 80, 80), F32),)
    )(parts, after)
    other = lax.ppermute(send, "zl", [(0, 1), (1, 0)])
    grads = call(last_sum_body, [sds((60, 80), F32), sds((20, 80), F32)], 2, 0)(own, other)
    return [grad.T for grad in grads]


def edges(top, bottom):
    low = lax.ppermute(bottom, "zh", [(i, (i + 1) % 4) for i in range(4)])
    high = lax.ppermute(top, "zh", [(i, (i + 3) % 4) for i in range(4)])
    return low, high


def exchange(rows):
    return lax.all_to_all(rows, FRAME, split_axis=0, concat_axis=0, tiled=True)


def shards(latents, space_kernel, time_kernel, qkv_weight, out_weight, norm_gain, grad_out):
    images, incoming = latents[0, 0], grad_out[0, 0]
    gain = norm_gain.reshape(1, C)
    half, twin, top, bottom = halves_of(time_kernel, qkv_weight, out_weight, images)
    others = round_trip([half] * 3, "y")
    low, high = edges(top, bottom)
    near = across(gate(twin, high))
    rows = conv_forward(images, low, high, incoming, space_kernel)
    tile = exchange(rows)
    own, three = four_of(half, others, rows, near)
    far = gate(across(three), tile)
    weights = [own, swapped(own), near, swapped(near), far, swapped(far)]
    temporal, normal, time, weight = temporal_step(tile, gain, weights)
    grad_packed, mixed, send = attention_step(normal, tile, weight)
    keep = own_gradient(normal, mixed, tile, grad_packed)
    summed = pair_sum(keep, send)
    grad_spatial = exchange(
        tile_gradient(grad_packed, temporal, tile, gain, weight, time, summed[0])
    )
    low, high = edges(grad_spatial[0:1], grad_spatial[7:8])
    grad_latents, token = conv_backward(grad_spatial, low, high, space_kernel)
    grad_qkv, grad_outproj = reduce_grads(summed, token)
    return grad_latents[None, None], grad_qkv, grad_outproj


def solution(mesh):
    inner = Mesh(mesh.devices.reshape(2, 4, 4, 2, 4), ("zl", "y", "x", "c", "zh"))
    tiles = P(VIDEO, FRAME, "zh", None, None)
    weight = P(VIDEO, None)
    grads = P(VIDEO, ("x", "c", "zh"))
    return jax.shard_map(
        shards,
        mesh=inner,
        in_specs=(tiles, P(), weight, weight, weight, P(), tiles),
        out_specs=(tiles, grads, grads),
        check_vma=False,
    )
```

```python
import functools

import jax
import jax.numpy as jnp
from jax import lax
from jax.experimental import pallas as pl
from jax.experimental.pallas import tpu as pltpu
from jax.sharding import Mesh
from jax.sharding import PartitionSpec as P

HEAD_DIM = 64
C = 640
F32 = jnp.float32
BF16 = jnp.bfloat16
VIDEO = ("zl", "y")
FRAME = ("x", "c")
MIB = 1 << 20
BLOCKS = (4, 4, 80, C)


def sds(shape, dtype=BF16):
    return jax.ShapeDtypeStruct(shape, dtype)


AXES = ("zl", "y", "x", "c", "zh")


def call(body, outs, n_vmem, n_any, scratch=(), limit=12, flops=0, moved=0):
    def placed_body(*refs):
        body([lax.axis_index(name) for name in AXES], *refs)

    specs = [pl.BlockSpec(memory_space=pltpu.VMEM)] * n_vmem
    specs += [pl.BlockSpec(memory_space=pl.ANY)] * n_any
    return pl.pallas_call(
        placed_body,
        out_shape=outs,
        in_specs=specs,
        out_specs=[pl.BlockSpec(memory_space=pltpu.VMEM)] * len(outs),
        scratch_shapes=list(scratch),
        compiler_params=pltpu.CompilerParams(vmem_limit_bytes=limit * MIB),
        cost_estimate=pl.CostEstimate(flops=flops, bytes_accessed=moved, transcendentals=0),
    )


def mm(a, b):
    return lax.dot_general(a, b, (((1,), (0,)), ((), ())), preferred_element_type=F32)


def mm_nt(a, b):
    return lax.dot_general(a, b, (((1,), (1,)), ((), ())), preferred_element_type=F32)


def mm_tn(a, b):
    return lax.dot_general(a, b, (((0,), (0,)), ((), ())), preferred_element_type=F32)


def shifted_columns(images_ref, low_ref, high_ref, zh, shifts_ref, order):
    low = low_ref[...].astype(F32) * jnp.where(zh > 0, 1.0, 0.0)
    high = high_ref[...].astype(F32) * jnp.where(zh < 3, 1.0, 0.0)
    whole = jnp.concatenate([low, images_ref[...].astype(F32), high], axis=0)
    flat = whole.reshape(320, C)
    column = lax.broadcasted_iota(jnp.int32, (320, C), 0) % 32
    before = jnp.where(column == 0, 0.0, pltpu.roll(flat, 1, 0))
    after = jnp.where(column == 31, 0.0, pltpu.roll(flat, 319, 0))
    views = (before, flat, after)
    for j, which in enumerate(order):
        shifts_ref[:, j * C : (j + 1) * C] = views[which].astype(BF16)


def kernel_copies(kernel_hbm, kernel_ref, sems):
    copies = []
    for dx in range(3):
        tap = (pl.ds(0, 1), pl.ds(dx, 1))
        copies.append(pltpu.make_async_copy(kernel_hbm.at[tap], kernel_ref.at[tap], sems.at[dx]))
    for dy in (1, 2):
        row = (pl.ds(dy, 1),)
        copies.append(pltpu.make_async_copy(kernel_hbm.at[row], kernel_ref.at[row], sems.at[dy + 2]))
    return copies


def conv_forward_body(pos, low, high, images_hbm, grad_hbm, kernel_hbm, out, *scratch):
    kernel_ref, shifts, sems, images, image_sems = scratch
    inputs = [
        pltpu.make_async_copy(images_hbm, images, image_sems.at[0]),
        pltpu.make_async_copy(grad_hbm, out.at[:, 1], image_sems.at[1]),
    ]
    copies = kernel_copies(kernel_hbm, kernel_ref, sems)
    for copy in inputs[:1] + copies + inputs[1:]:
        copy.start()
    inputs[0].wait()
    shifted_columns(images, low, high, pos[4], shifts, (0, 1, 2))
    total = images[...].astype(F32).reshape(256, C)
    for dx in range(3):
        copies[dx].wait()
        total = total + mm(shifts[0:256, dx * C : (dx + 1) * C], kernel_ref[0, dx])
    for dy in (1, 2):
        copies[dy + 2].wait()
        taps = kernel_ref[dy].reshape(3 * C, C)
        total = total + mm(shifts[32 * dy : 32 * dy + 256, :], taps)
    out[:, 0] = total.astype(BF16).reshape(8, 32, C)
    inputs[1].wait()


def conv_backward_body(pos, images, low, high, kernel_hbm, out, token, kernel_ref, shifts, sems):
    token[...] = jnp.zeros((8, 128), F32)
    copies = kernel_copies(kernel_hbm, kernel_ref, sems)
    for copy in copies:
        copy.start()
    shifted_columns(images, low, high, pos[4], shifts, (2, 1, 0))
    total = images[...].astype(F32).reshape(256, C)
    for dy in range(3):
        at = 32 * (2 - dy)
        if dy > 0:
            copies[dy + 2].wait()
        for dx in range(3):
            if dy == 0:
                copies[dx].wait()
            total = total + mm_nt(shifts[at : at + 256, dx * C : (dx + 1) * C], kernel_ref[dy, dx])
    out[...] = total.astype(BF16).reshape(8, 32, C)


CONV_SCRATCH = (pltpu.VMEM((3, 3, C, C), BF16), pltpu.VMEM((320, 3 * C), BF16))


def conv_forward(images, low, high, grad_out, kernel):
    return call(
        conv_forward_body,
        [sds((8, 2, 32, C))],
        2,
        3,
        CONV_SCRATCH
        + (
            pltpu.SemaphoreType.DMA((5,)),
            pltpu.VMEM((8, 32, C), BF16),
            pltpu.SemaphoreType.DMA((2,)),
        ),
        limit=48,
        flops=2 * 256 * 9 * C * C,
        moved=9 * C * C * 2,
    )(low, high, images, grad_out, kernel)[0]


def conv_backward(images, low, high, kernel):
    return call(
        conv_backward_body,
        [sds((8, 32, C)), sds((8, 128), F32)],
        3,
        1,
        CONV_SCRATCH + (pltpu.SemaphoreType.DMA((5,)),),
        limit=48,
        flops=2 * 256 * 9 * C * C,
        moved=9 * C * C * 2,
    )(images, low, high, kernel)


def halves_body(pos, time, qkv, out, images, half, twin, top, bottom, sems):
    core = pos[3]
    rows = time.at[pl.ds(pl.multiple_of(112 * core, 16), 128)]

    def run(first, second):
        moves = [(images.at[pl.ds(0, 1)], top), (images.at[pl.ds(7, 1)], bottom)]
        for target in (half, twin):
            moves.append((rows, target.at[0:128]))
            moves.append((first, target.at[128:208]))
            moves.append((second, target.at[208:288]))
        copies = [pltpu.make_async_copy(a, b, sems.at[i]) for i, (a, b) in enumerate(moves)]
        for copy in copies:
            copy.start()
        for copy in copies:
            copy.wait()

    @pl.when(core == 0)
    def _():
        run(qkv.at[:, 0:C], qkv.at[:, C : 2 * C])

    @pl.when(core == 1)
    def _():
        run(qkv.at[:, 2 * C : 3 * C], out)


def halves_of(time, qkv, out, images):
    dma = (pltpu.SemaphoreType.DMA((8,)),)
    outs = [sds((288, C))] * 2 + [sds((1, 32, C))] * 2
    return call(halves_body, outs, 0, 4, dma, limit=62)(time, qkv, out, images)


def gate(value, after):
    return pl.pallas_call(
        lambda a, b, c: None,
        out_shape=sds(value.shape, value.dtype),
        in_specs=[pl.BlockSpec(memory_space=pl.ANY)] * 2,
        out_specs=pl.BlockSpec(memory_space=pl.ANY),
        input_output_aliases={0: 0},
        compiler_params=pltpu.CompilerParams(vmem_limit_bytes=MIB),
    )(value, after)


def four_body(pos, own, *refs):
    others, four, three = refs[:3], refs[-2], refs[-1]
    four[pos[1]] = own[...]
    for k in range(3):
        four[(pos[1] + 3 - k) % 4] = others[k][...]
        three[k] = others[k][...]


def four_of(own, others, *after):
    outs = [sds((4,) + own.shape), sds((3,) + own.shape)]
    return call(four_body, outs, 4, len(after))(own, *others, *after)


def across(own):
    pairs = []
    for z in range(8):
        for core in range(2):
            to = (z + 7 + 2 * core) % 8
            pairs.append(tuple(((at % 2) * 2 + core) * 4 + at // 2 for at in (z, to)))
    return lax.ppermute(own, ("zl", "c", "zh"), pairs)


def swapped(value):
    return lax.ppermute(value, "c", [(0, 1), (1, 0)])


def placed_pieces(pos, pieces):
    zl, y, core = pos[0], pos[1], pos[3]
    own, own_swapped, near, near_swapped, three, three_swapped = pieces
    placed = [(own, pl.ds(4 * zl, 4), core), (own_swapped, pl.ds(4 * zl, 4), 1 - core)]
    for half, one, others in ((core, near, three), (1 - core, near_swapped, three_swapped)):
        placed.append((one, 4 * (1 - zl) + y, half))
        for k in range(3):
            placed.append((others.at[k], 4 * (1 - zl) + (y + 3 - k) % 4, half))
    return placed


def time_copies(pos, pieces, target, sem):
    copies = []
    for i, (piece, blocks, half) in enumerate(placed_pieces(pos, pieces)):
        lead = (slice(None),) if i < 2 else ()

        def part(first, last, n, i=i, piece=piece, blocks=blocks, lead=lead):
            source = piece.at[lead + (pl.ds(pl.multiple_of(first, 16), n),)]
            place = target.at[blocks, pl.ds(pl.multiple_of(last, 16), n)]
            copies.append(pltpu.make_async_copy(source, place, sem.at[len(copies)]))

        part(16 * half, 128 * half, 112)
        if i == 0 or 2 <= i < 6:
            part(112 * (1 - half), 112, 16)
    return copies


def projection_copies(pos, pieces, target, sem):
    copies = []
    for i, (piece, blocks, half) in enumerate(placed_pieces(pos, pieces)):
        lead = (slice(None),) if i < 2 else ()
        for j in range(2):
            lanes = pl.ds(pl.multiple_of(1280 * half + 640 * j, 128), 640)
            source = piece.at[lead + (pl.ds(128 + 80 * j, 80),)]
            place = target.at[blocks, :, lanes]
            copies.append(pltpu.make_async_copy(source, place, sem.at[2 * i + j]))
    return copies


def temporal_body(pos, tile, gain, *refs):
    pieces, (temporal_out, normal_out, time_ref, weight_ref) = refs[:6], refs[6:10]
    padded, sem, weight_sem = refs[10:]
    copies = time_copies(pos, pieces, time_ref, sem)
    later_copies = projection_copies(pos, pieces, weight_ref, weight_sem)
    for copy in copies + later_copies:
        copy.start()
    value = tile[:, 0].astype(F32)
    padded[0] = jnp.zeros((32, C), BF16)
    padded[1:9] = (value * jax.nn.sigmoid(value)).astype(BF16)
    padded[9] = jnp.zeros((32, C), BF16)
    total = value.reshape(256, C)
    for copy in copies:
        copy.wait()
    taps = time_ref[...].reshape(3 * C, C)
    for k in range(3):
        total = total + mm(padded[k : k + 8].reshape(256, C), taps[k * C : (k + 1) * C, :])
    temporal = total.astype(BF16)
    temporal_out[...] = temporal
    value = temporal.astype(F32)
    scale = lax.rsqrt(jnp.mean(value * value, axis=-1, keepdims=True) + 1e-06)
    normal_out[...] = (value * scale * gain[...]).astype(BF16)
    for copy in later_copies:
        copy.wait()


PADDED = (pltpu.VMEM((10, 32, C), BF16),)


def temporal_step(tile, gain, pieces):
    return call(
        temporal_body,
        [sds((256, C)), sds((256, C)), sds((8, 240, C)), sds((8, 80, 4 * C))],
        2,
        6,
        PADDED + (pltpu.SemaphoreType.DMA((15,)), pltpu.SemaphoreType.DMA((20,))),
        limit=24,
        flops=2 * 256 * 3 * C * C,
        moved=3 * C * C * 2,
    )(tile, gain, *pieces)


def attention_body(pos, normal, tile, weight_ref, grad_packed, mixed_out, send, *scratch):
    packed, grad_blend, blended = scratch
    weight = weight_ref[...].reshape(C, 4 * C)
    packed[...] = mm(normal[...], weight[:, : 3 * C]).astype(BF16).reshape(8, 2, 16, 3 * C)
    grad_blend[...] = mm_nt(tile[:, 1].reshape(256, C), weight[:, 3 * C :]).astype(BF16).reshape(8, 2, 16, C)
    first_head = lax.broadcasted_iota(jnp.int32, (128, 128), 1) < HEAD_DIM
    row_pixel = lax.broadcasted_iota(jnp.int32, (256, 128), 0) % 16
    column_pixel = lax.broadcasted_iota(jnp.int32, (256, 128), 1) % 16
    same_pixel = row_pixel == column_pixel
    nothing = jnp.zeros((128, 128), BF16)

    def two_heads(block):
        return jnp.concatenate(
            [jnp.where(first_head, block, nothing), jnp.where(first_head, nothing, block)], axis=0
        )

    def merged(both):
        return jnp.where(first_head, both[:128], both[128:]).astype(BF16)

    blocks = [(half, pair * 128) for pair in range(5) for half in range(2)]

    def parts(ref, offset):
        return [
            ref[:, half, :, offset + at : offset + at + 128].reshape(128, 128)
            for half, at in blocks
        ]

    def each(function, *lists):
        return [function(*values) for values in zip(*lists)]

    def row_sum(values):
        return jnp.sum(values, axis=-1, keepdims=True)

    queries = each(two_heads, parts(packed, 0))
    keys, values = parts(packed, C), parts(packed, 2 * C)
    upper = each(two_heads, parts(grad_blend, 0))
    scores = each(mm_nt, queries, keys)
    grad_probs = each(mm_nt, upper, values)
    scores = each(lambda s: jnp.where(same_pixel, s * HEAD_DIM**-0.5, -1e30), scores)
    largest = each(lambda s: jnp.max(s, axis=-1, keepdims=True), scores)
    expons = each(lambda s, top: jnp.exp(s - top), scores, largest)
    probs = each(lambda e, total: e * (1.0 / total), expons, each(row_sum, expons))
    rounded = each(lambda p: p.astype(BF16), probs)
    inner = each(lambda g, p: row_sum(g * p), grad_probs, probs)
    grad_scores = each(
        lambda p, g, i: (p * (g - i) * HEAD_DIM**-0.5).astype(BF16), probs, grad_probs, inner
    )
    mixed = each(lambda p, v: merged(mm(p, v)), rounded, values)
    results = (
        each(lambda g, k: merged(mm(g, k)), grad_scores, keys),
        each(lambda g, q: mm_tn(g, q).astype(BF16), grad_scores, queries),
        each(lambda p, u: mm_tn(p, u).astype(BF16), rounded, upper),
    )
    for n, (half, at) in enumerate(blocks):
        blended[:, half, :, at : at + 128] = mixed[n].reshape(8, 16, 128)
        for i in range(3):
            lanes = slice(i * C + at, i * C + at + 128)
            grad_packed[:, half, :, lanes] = results[i][n].reshape(8, 16, 128)

    mixed_out[...] = blended[...].reshape(256, C)
    weight_gradient(1 - pos[3], normal, mixed_out, tile, grad_packed, send)


def gradient_pair(first, second):
    def gap(n):
        return jnp.zeros((256, n), BF16)

    def placed(left, *parts):
        return mm_tn(left, jnp.concatenate(parts, axis=1))

    a = placed(first[0], first[2], gap(16))
    b = placed(first[1], gap(112), first[3], gap(64))
    c = placed(second[0], gap(64), second[2], gap(80))
    d = placed(second[1], gap(48), second[3])
    groups = (
        a[:, :128],
        a[:, 128:] + b[:, :128],
        b[:, 128:] + c[:, :128],
        c[:, 128:256],
        c[:, 256:] + d,
    )
    return jnp.concatenate(groups, axis=1).astype(BF16)


def weight_gradient(core, normal, mixed, tile, grad_packed, target):
    for which in range(2):

        @pl.when(core == which)
        def _(which=which):
            packed = grad_packed[...].reshape(256, 3 * C)
            arriving = tile[:, 1].reshape(256, C)
            left, right = normal[...], mixed[...]

            def sides(x):
                at = 2 * x + which
                return packed[:, 240 * at : 240 * at + 240], arriving[:, 80 * at : 80 * at + 80]

            if which == 0:
                for half in range(2):
                    a, b = [(left, right) + sides(2 * half + i) for i in range(2)]
                    both = gradient_pair(a, b).reshape(2, 4, 80, C)
                    for zl in range(2):
                        target[:, 2 * zl + half] = both[zl]
            else:
                lefts = left[:, :320], left[:, 320:]
                rights = right[:, :320], right[:, 320:]
                for x in range(4):
                    a, b = [(lefts[zl], rights[zl]) + sides(x) for zl in range(2)]
                    target[x] = gradient_pair(a, b).reshape(4, 80, C)


def own_gradient_body(pos, normal, mixed, tile, grad_packed, keep):
    weight_gradient(pos[3], normal, mixed, tile, grad_packed, keep)


def own_gradient(normal, mixed, tile, grad_packed):
    return call(
        own_gradient_body,
        [sds(BLOCKS)],
        4,
        0,
        limit=24,
        flops=2 * 256 * 2 * C * C,
        moved=2 * C * C * 2,
    )(normal, mixed, tile, grad_packed)[0]


def attention_step(normal, tile, weight):
    return call(
        attention_body,
        [sds((8, 2, 16, 3 * C)), sds((256, C)), sds(BLOCKS)],
        3,
        0,
        (
            pltpu.VMEM((8, 2, 16, 3 * C), BF16),
            pltpu.VMEM((8, 2, 16, C), BF16),
            pltpu.VMEM((8, 2, 16, C), BF16),
        ),
        limit=32,
        flops=2 * 256 * 8 * C * C,
        moved=4 * C * C * 2,
    )(normal, tile, weight)


def tile_gradient_body(pos, *refs):
    grad_packed, temporal, tile, gain, weight_ref, time_ref, _, out, padded = refs
    weight = weight_ref[...].reshape(C, 4 * C)[:, : 3 * C]
    grad_normal = mm_nt(grad_packed[...].reshape(256, 3 * C), weight)
    value = temporal[...].astype(F32)
    scale = lax.rsqrt(jnp.mean(value * value, axis=-1, keepdims=True) + 1e-06)
    scaled = grad_normal * gain[...]
    inner = jnp.mean(value * scaled, axis=-1, keepdims=True)
    through_norm = scale * scaled - value * (scale * scale * scale * inner)
    grad_temporal = (tile[:, 1].astype(F32).reshape(256, C) + through_norm).astype(BF16)
    padded[0] = jnp.zeros((32, C), BF16)
    padded[1:9] = grad_temporal.reshape(8, 32, C)
    padded[9] = jnp.zeros((32, C), BF16)
    taps = time_ref[...].reshape(3 * C, C)
    grad_act = jnp.zeros((256, C), F32)
    for k in range(3):
        later = padded[2 - k : 10 - k].reshape(256, C)
        grad_act = grad_act + mm_nt(later, taps[k * C : (k + 1) * C, :])
    as_float = tile[:, 0].astype(F32).reshape(256, C)
    logistic = jax.nn.sigmoid(as_float)
    grad_spatial = grad_temporal.astype(F32) + grad_act * logistic * (
        1.0 + as_float * (1.0 - logistic)
    )
    out[...] = grad_spatial.astype(BF16).reshape(8, 32, C)


def tile_gradient(grad_packed, temporal, tile, gain, weight, time, after):
    return call(
        tile_gradient_body,
        [sds((8, 32, C))],
        6,
        1,
        PADDED,
        limit=24,
        flops=2 * 256 * 6 * C * C,
        moved=7 * C * C * 2,
    )(grad_packed, temporal, tile, gain, weight, time, after)[0]


def pair_sum_body(pos, keep, other, own, *sends):
    me = jnp.where(pos[3] == 0, pos[1], pos[2])

    def block(index):
        return keep[index].astype(F32) + other[index].astype(F32)

    own[...] = block(me)
    for k in range(3):
        sends[k][...] = block((me + k + 1) % 4).astype(BF16)


def second_sum_body(pos, held, *refs):
    others, own, sends, scratch = refs[0:3], refs[3], refs[4:7], refs[7]
    total = held[...]
    for other in others:
        total = total + other[...].astype(F32)

    for which in range(2):

        @pl.when(pos[3] == which)
        def _(which=which):
            for i in range(4):
                for zl in range(2):
                    block, at = (2 * zl + i // 2, i % 2) if which == 0 else (i, zl)
                    scratch[i, zl] = total[block, :, 320 * at : 320 * at + 320]

    me = jnp.where(pos[3] == 0, pos[2], pos[1])
    own[...] = scratch[me]
    for k in range(3):
        sends[k][...] = scratch[(me + k + 1) % 4].astype(BF16)


def third_sum_body(pos, held, first, second, third, out):
    total = held[...]
    for other in (first, second, third):
        total = total + other[...].astype(F32)
    for row in range(4):
        out[row, :, :, 0:60] = total[:, :, 60 * row : 60 * row + 60].astype(BF16)
        out[row, :, :, 60:80] = total[:, :, 240 + 20 * row : 240 + 20 * row + 20].astype(BF16)


def row_sum_body(pos, parts, after, own, send, scratch):
    scratch[...] = jnp.sum(parts[...].astype(F32), axis=0)
    own[...] = scratch[pos[0]]
    send[...] = scratch[1 - pos[0]].astype(BF16)


def last_sum_body(pos, held, other, qkv_out, out_out):
    total = (held[...] + other[...].astype(F32)).T
    qkv_out[...] = total[0:60]
    out_out[...] = total[60:80]


def round_trip(sends, axis):
    return [
        lax.ppermute(sends[k], axis, [(i, (i + k + 1) % 4) for i in range(4)]) for k in range(3)
    ]


def crosswise(sends, first):
    def target(y, x, core, k):
        if (core == 0) == first:
            return (y + k + 1) % 4, x
        return y, (x + k + 1) % 4

    moved = []
    for k in range(3):
        pairs = []
        for y in range(4):
            for x in range(4):
                for core in range(2):
                    ty, tx = target(y, x, core, k)
                    pairs.append(((y * 4 + x) * 2 + core, (ty * 4 + tx) * 2 + core))
        moved.append(lax.ppermute(sends[k], ("y", "x", "c"), pairs))
    return moved


def pair_sum(keep, send):
    step = BLOCKS[1:]
    return call(pair_sum_body, [sds(step, F32)] + [sds(step)] * 3, 2, 0, limit=20)(
        keep, swapped(send)
    )


def reduce_grads(summed, after):
    own, *sends = summed
    step = (2, 80, 320)
    own, *sends = call(
        second_sum_body,
        [sds(step, F32)] + [sds(step)] * 3,
        4,
        0,
        (pltpu.VMEM((4,) + step, F32),),
        limit=20,
    )(own, *crosswise(sends, True))
    parts = call(third_sum_body, [sds((4, 2, 80, 80))], 4, 0)(own, *crosswise(sends, False))[0]
    parts = lax.all_to_all(parts, "zh", split_axis=0, concat_axis=0, tiled=True)
    own, send = call(
        row_sum_body, [sds((80, 80), F32), sds((80, 80))], 1, 1, (pltpu.VMEM((2, 80, 80), F32),)
    )(parts, after)
    other = lax.ppermute(send, "zl", [(0, 1), (1, 0)])
    grads = call(last_sum_body, [sds((60, 80), F32), sds((20, 80), F32)], 2, 0)(own, other)
    return [grad.T for grad in grads]


def edges(top, bottom):
    low = lax.ppermute(bottom, "zh", [(i, (i + 1) % 4) for i in range(4)])
    high = lax.ppermute(top, "zh", [(i, (i + 3) % 4) for i in range(4)])
    return low, high


def exchange(rows):
    return lax.all_to_all(rows, FRAME, split_axis=0, concat_axis=0, tiled=True)


def shards(latents, space_kernel, time_kernel, qkv_weight, out_weight, norm_gain, grad_out):
    images, incoming = latents[0, 0], grad_out[0, 0]
    gain = norm_gain.reshape(1, C)
    half, twin, top, bottom = halves_of(time_kernel, qkv_weight, out_weight, images)
    others = round_trip([half] * 3, "y")
    low, high = edges(top, bottom)
    near = across(gate(twin, high))
    rows = conv_forward(images, low, high, incoming, space_kernel)
    tile = exchange(rows)
    own, three = four_of(half, others, rows, near)
    far = gate(across(three), tile)
    weights = [own, swapped(own), near, swapped(near), far, swapped(far)]
    temporal, normal, time, weight = temporal_step(tile, gain, weights)
    grad_packed, mixed, send = attention_step(normal, tile, weight)
    keep = own_gradient(normal, mixed, tile, grad_packed)
    summed = pair_sum(keep, send)
    grad_spatial = exchange(
        tile_gradient(grad_packed, temporal, tile, gain, weight, time, summed[0])
    )
    low, high = edges(grad_spatial[0:1], grad_spatial[7:8])
    grad_latents, token = conv_backward(grad_spatial, low, high, space_kernel)
    grad_qkv, grad_outproj = reduce_grads(summed, token)
    return grad_latents[None, None], grad_qkv, grad_outproj


def solution(mesh):
    inner = Mesh(mesh.devices.reshape(2, 4, 4, 2, 4), ("zl", "y", "x", "c", "zh"))
    tiles = P(VIDEO, FRAME, "zh", None, None)
    weight = P(VIDEO, None)
    grads = P(VIDEO, ("x", "c", "zh"))
    return jax.shard_map(
        shards,
        mesh=inner,
        in_specs=(tiles, P(), weight, weight, weight, P(), tiles),
        out_specs=(tiles, grads, grads),
        check_vma=False,
    )
```

```python
import functools

import jax
import jax.numpy as jnp
from jax import lax
from jax.experimental import pallas as pl
from jax.experimental.pallas import tpu as pltpu
from jax.sharding import Mesh
from jax.sharding import PartitionSpec as P

HEAD_DIM = 64
C = 640
F32 = jnp.float32
BF16 = jnp.bfloat16
VIDEO = ("zl", "y")
FRAME = ("x", "c")
MIB = 1 << 20
BLOCKS = (4, 4, 80, C)


def sds(shape, dtype=BF16):
    return jax.ShapeDtypeStruct(shape, dtype)


AXES = ("zl", "y", "x", "c", "zh")


def call(body, outs, n_vmem, n_any, scratch=(), limit=12, flops=0, moved=0):
    def placed_body(*refs):
        body([lax.axis_index(name) for name in AXES], *refs)

    specs = [pl.BlockSpec(memory_space=pltpu.VMEM)] * n_vmem
    specs += [pl.BlockSpec(memory_space=pl.ANY)] * n_any
    return pl.pallas_call(
        placed_body,
        out_shape=outs,
        in_specs=specs,
        out_specs=[pl.BlockSpec(memory_space=pltpu.VMEM)] * len(outs),
        scratch_shapes=list(scratch),
        compiler_params=pltpu.CompilerParams(vmem_limit_bytes=limit * MIB),
        cost_estimate=pl.CostEstimate(flops=flops, bytes_accessed=moved, transcendentals=0),
    )


def mm(a, b):
    return lax.dot_general(a, b, (((1,), (0,)), ((), ())), preferred_element_type=F32)


def mm_nt(a, b):
    return lax.dot_general(a, b, (((1,), (1,)), ((), ())), preferred_element_type=F32)


def mm_tn(a, b):
    return lax.dot_general(a, b, (((0,), (0,)), ((), ())), preferred_element_type=F32)


def shifted_columns(images_ref, low_ref, high_ref, zh, shifts_ref, order):
    low = low_ref[...].astype(F32) * jnp.where(zh > 0, 1.0, 0.0)
    high = high_ref[...].astype(F32) * jnp.where(zh < 3, 1.0, 0.0)
    whole = jnp.concatenate([low, images_ref[...].astype(F32), high], axis=0)
    flat = whole.reshape(320, C)
    column = lax.broadcasted_iota(jnp.int32, (320, C), 0) % 32
    before = jnp.where(column == 0, 0.0, pltpu.roll(flat, 1, 0))
    after = jnp.where(column == 31, 0.0, pltpu.roll(flat, 319, 0))
    views = (before, flat, after)
    for j, which in enumerate(order):
        shifts_ref[:, j * C : (j + 1) * C] = views[which].astype(BF16)


def kernel_copies(kernel_hbm, kernel_ref, sems):
    copies = []
    for dx in range(3):
        tap = (pl.ds(0, 1), pl.ds(dx, 1))
        copies.append(pltpu.make_async_copy(kernel_hbm.at[tap], kernel_ref.at[tap], sems.at[dx]))
    for dy in (1, 2):
        row = (pl.ds(dy, 1),)
        copies.append(pltpu.make_async_copy(kernel_hbm.at[row], kernel_ref.at[row], sems.at[dy + 2]))
    return copies


def conv_forward_body(pos, low, high, images_hbm, grad_hbm, kernel_hbm, out, *scratch):
    kernel_ref, shifts, sems, images, image_sems = scratch
    inputs = [
        pltpu.make_async_copy(images_hbm, images, image_sems.at[0]),
        pltpu.make_async_copy(grad_hbm, out.at[:, 1], image_sems.at[1]),
    ]
    copies = kernel_copies(kernel_hbm, kernel_ref, sems)
    for copy in inputs[:1] + copies + inputs[1:]:
        copy.start()
    inputs[0].wait()
    shifted_columns(images, low, high, pos[4], shifts, (0, 1, 2))
    total = images[...].astype(F32).reshape(256, C)
    for dx in range(3):
        copies[dx].wait()
        total = total + mm(shifts[0:256, dx * C : (dx + 1) * C], kernel_ref[0, dx])
    for dy in (1, 2):
        copies[dy + 2].wait()
        taps = kernel_ref[dy].reshape(3 * C, C)
        total = total + mm(shifts[32 * dy : 32 * dy + 256, :], taps)
    out[:, 0] = total.astype(BF16).reshape(8, 32, C)
    inputs[1].wait()


def conv_backward_body(pos, images, low, high, kernel_hbm, out, token, kernel_ref, shifts, sems):
    token[...] = jnp.zeros((8, 128), F32)
    copies = kernel_copies(kernel_hbm, kernel_ref, sems)
    for copy in copies:
        copy.start()
    shifted_columns(images, low, high, pos[4], shifts, (2, 1, 0))
    total = images[...].astype(F32).reshape(256, C)
    for dy in range(3):
        at = 32 * (2 - dy)
        if dy > 0:
            copies[dy + 2].wait()
        for dx in range(3):
            if dy == 0:
                copies[dx].wait()
            total = total + mm_nt(shifts[at : at + 256, dx * C : (dx + 1) * C], kernel_ref[dy, dx])
    out[...] = total.astype(BF16).reshape(8, 32, C)


CONV_SCRATCH = (pltpu.VMEM((3, 3, C, C), BF16), pltpu.VMEM((320, 3 * C), BF16))


def conv_forward(images, low, high, grad_out, kernel):
    return call(
        conv_forward_body,
        [sds((8, 2, 32, C))],
        2,
        3,
        CONV_SCRATCH
        + (
            pltpu.SemaphoreType.DMA((5,)),
            pltpu.VMEM((8, 32, C), BF16),
            pltpu.SemaphoreType.DMA((2,)),
        ),
        limit=48,
        flops=2 * 256 * 9 * C * C,
        moved=9 * C * C * 2,
    )(low, high, images, grad_out, kernel)[0]


def conv_backward(images, low, high, kernel):
    return call(
        conv_backward_body,
        [sds((8, 32, C)), sds((8, 128), F32)],
        3,
        1,
        CONV_SCRATCH + (pltpu.SemaphoreType.DMA((5,)),),
        limit=48,
        flops=2 * 256 * 9 * C * C,
        moved=9 * C * C * 2,
    )(images, low, high, kernel)


def halves_body(pos, time, qkv, out, images, half, twin, top, bottom, sems):
    core = pos[3]
    rows = time.at[pl.ds(pl.multiple_of(112 * core, 16), 128)]

    def run(first, second):
        moves = [(images.at[pl.ds(0, 1)], top), (images.at[pl.ds(7, 1)], bottom)]
        for target in (half, twin):
            moves.append((rows, target.at[0:128]))
            moves.append((first, target.at[128:208]))
            moves.append((second, target.at[208:288]))
        copies = [pltpu.make_async_copy(a, b, sems.at[i]) for i, (a, b) in enumerate(moves)]
        for copy in copies:
            copy.start()
        for copy in copies:
            copy.wait()

    @pl.when(core == 0)
    def _():
        run(qkv.at[:, 0:C], qkv.at[:, C : 2 * C])

    @pl.when(core == 1)
    def _():
        run(qkv.at[:, 2 * C : 3 * C], out)


def halves_of(time, qkv, out, images):
    dma = (pltpu.SemaphoreType.DMA((8,)),)
    outs = [sds((288, C))] * 2 + [sds((1, 32, C))] * 2
    return call(halves_body, outs, 0, 4, dma, limit=62)(time, qkv, out, images)


def gate(value, after):
    return pl.pallas_call(
        lambda a, b, c: None,
        out_shape=sds(value.shape, value.dtype),
        in_specs=[pl.BlockSpec(memory_space=pl.ANY)] * 2,
        out_specs=pl.BlockSpec(memory_space=pl.ANY),
        input_output_aliases={0: 0},
        compiler_params=pltpu.CompilerParams(vmem_limit_bytes=MIB),
    )(value, after)


def four_body(own, first, second, third, *refs):
    four, three, sems = refs[-3:]
    y = lax.axis_index("y")
    copies = [pltpu.make_async_copy(own, four.at[y], sems.at[3])]
    for k, other in enumerate((first, second, third)):
        copies.append(pltpu.make_async_copy(other, four.at[(y + 3 - k) % 4], sems.at[k]))
    for copy in copies:
        copy.start()
    for k, other in enumerate((first, second, third)):
        three[k] = other[...]
    for copy in copies:
        copy.wait()


def four_of(own, others, *after):
    vmem, anywhere = pl.BlockSpec(memory_space=pltpu.VMEM), pl.BlockSpec(memory_space=pl.ANY)
    return pl.pallas_call(
        four_body,
        out_shape=[sds((4,) + own.shape), sds((3,) + own.shape)],
        in_specs=[vmem] * 4 + [anywhere] * len(after),
        out_specs=[pl.BlockSpec(memory_space=pltpu.HBM), vmem],
        scratch_shapes=[pltpu.SemaphoreType.DMA((4,))],
        compiler_params=pltpu.CompilerParams(vmem_limit_bytes=12 * MIB),
    )(own, *others, *after)


def across(own):
    pairs = []
    for z in range(8):
        for core in range(2):
            to = (z + 7 + 2 * core) % 8
            pairs.append(tuple(((at % 2) * 2 + core) * 4 + at // 2 for at in (z, to)))
    return lax.ppermute(own, ("zl", "c", "zh"), pairs)


def swapped(value):
    return lax.ppermute(value, "c", [(0, 1), (1, 0)])


def placed_pieces(pos, pieces):
    zl, y, core = pos[0], pos[1], pos[3]
    own, own_swapped, near, near_swapped, three, three_swapped = pieces
    placed = [(own, pl.ds(4 * zl, 4), core), (own_swapped, pl.ds(4 * zl, 4), 1 - core)]
    for half, one, others in ((core, near, three), (1 - core, near_swapped, three_swapped)):
        placed.append((one, 4 * (1 - zl) + y, half))
        for k in range(3):
            placed.append((others.at[k], 4 * (1 - zl) + (y + 3 - k) % 4, half))
    return placed


def time_copies(pos, pieces, target, sem):
    copies = []
    for i, (piece, blocks, half) in enumerate(placed_pieces(pos, pieces)):
        lead = (slice(None),) if i < 2 else ()

        def part(first, last, n, i=i, piece=piece, blocks=blocks, lead=lead):
            source = piece.at[lead + (pl.ds(pl.multiple_of(first, 16), n),)]
            place = target.at[blocks, pl.ds(pl.multiple_of(last, 16), n)]
            copies.append(pltpu.make_async_copy(source, place, sem.at[len(copies)]))

        part(16 * half, 128 * half, 112)
        if i == 0 or 2 <= i < 6:
            part(112 * (1 - half), 112, 16)
    return copies


def projection_copies(pos, pieces, target, sem):
    copies = []
    for i, (piece, blocks, half) in enumerate(placed_pieces(pos, pieces)):
        lead = (slice(None),) if i < 2 else ()
        for j in range(2):
            lanes = pl.ds(pl.multiple_of(1280 * half + 640 * j, 128), 640)
            source = piece.at[lead + (pl.ds(128 + 80 * j, 80),)]
            place = target.at[blocks, :, lanes]
            copies.append(pltpu.make_async_copy(source, place, sem.at[2 * i + j]))
    return copies


def temporal_body(pos, tile, gain, *refs):
    pieces, (temporal_out, normal_out, time_ref, weight_ref) = refs[:6], refs[6:10]
    padded, sem, weight_sem = refs[10:]
    copies = time_copies(pos, pieces, time_ref, sem)
    later_copies = projection_copies(pos, pieces, weight_ref, weight_sem)
    for copy in copies + later_copies:
        copy.start()
    value = tile[:, 0].astype(F32)
    padded[0] = jnp.zeros((32, C), BF16)
    padded[1:9] = (value * jax.nn.sigmoid(value)).astype(BF16)
    padded[9] = jnp.zeros((32, C), BF16)
    total = value.reshape(256, C)
    for copy in copies:
        copy.wait()
    taps = time_ref[...].reshape(3 * C, C)
    for k in range(3):
        total = total + mm(padded[k : k + 8].reshape(256, C), taps[k * C : (k + 1) * C, :])
    temporal = total.astype(BF16)
    temporal_out[...] = temporal
    value = temporal.astype(F32)
    scale = lax.rsqrt(jnp.mean(value * value, axis=-1, keepdims=True) + 1e-06)
    normal_out[...] = (value * scale * gain[...]).astype(BF16)
    for copy in later_copies:
        copy.wait()


PADDED = (pltpu.VMEM((10, 32, C), BF16),)


def temporal_step(tile, gain, pieces):
    return call(
        temporal_body,
        [sds((256, C)), sds((256, C)), sds((8, 240, C)), sds((8, 80, 4 * C))],
        2,
        6,
        PADDED + (pltpu.SemaphoreType.DMA((15,)), pltpu.SemaphoreType.DMA((20,))),
        limit=24,
        flops=2 * 256 * 3 * C * C,
        moved=3 * C * C * 2,
    )(tile, gain, *pieces)


def attention_body(pos, normal, tile, weight_ref, grad_packed, mixed_out, send, *scratch):
    packed, grad_blend, blended = scratch
    weight = weight_ref[...].reshape(C, 4 * C)
    packed[...] = mm(normal[...], weight[:, : 3 * C]).astype(BF16).reshape(8, 2, 16, 3 * C)
    grad_blend[...] = mm_nt(tile[:, 1].reshape(256, C), weight[:, 3 * C :]).astype(BF16).reshape(8, 2, 16, C)
    first_head = lax.broadcasted_iota(jnp.int32, (128, 128), 1) < HEAD_DIM
    row_pixel = lax.broadcasted_iota(jnp.int32, (256, 128), 0) % 16
    column_pixel = lax.broadcasted_iota(jnp.int32, (256, 128), 1) % 16
    same_pixel = row_pixel == column_pixel
    nothing = jnp.zeros((128, 128), BF16)

    def two_heads(block):
        return jnp.concatenate(
            [jnp.where(first_head, block, nothing), jnp.where(first_head, nothing, block)], axis=0
        )

    def merged(both):
        return jnp.where(first_head, both[:128], both[128:]).astype(BF16)

    blocks = [(half, pair * 128) for pair in range(5) for half in range(2)]

    def parts(ref, offset):
        return [
            ref[:, half, :, offset + at : offset + at + 128].reshape(128, 128)
            for half, at in blocks
        ]

    def each(function, *lists):
        return [function(*values) for values in zip(*lists)]

    def row_sum(values):
        return jnp.sum(values, axis=-1, keepdims=True)

    queries = each(two_heads, parts(packed, 0))
    keys, values = parts(packed, C), parts(packed, 2 * C)
    upper = each(two_heads, parts(grad_blend, 0))
    scores = each(mm_nt, queries, keys)
    grad_probs = each(mm_nt, upper, values)
    scores = each(lambda s: jnp.where(same_pixel, s * HEAD_DIM**-0.5, -1e30), scores)
    largest = each(lambda s: jnp.max(s, axis=-1, keepdims=True), scores)
    expons = each(lambda s, top: jnp.exp(s - top), scores, largest)
    probs = each(lambda e, total: e * (1.0 / total), expons, each(row_sum, expons))
    rounded = each(lambda p: p.astype(BF16), probs)
    inner = each(lambda g, p: row_sum(g * p), grad_probs, probs)
    grad_scores = each(
        lambda p, g, i: (p * (g - i) * HEAD_DIM**-0.5).astype(BF16), probs, grad_probs, inner
    )
    mixed = each(lambda p, v: merged(mm(p, v)), rounded, values)
    results = (
        each(lambda g, k: merged(mm(g, k)), grad_scores, keys),
        each(lambda g, q: mm_tn(g, q).astype(BF16), grad_scores, queries),
        each(lambda p, u: mm_tn(p, u).astype(BF16), rounded, upper),
    )
    for n, (half, at) in enumerate(blocks):
        blended[:, half, :, at : at + 128] = mixed[n].reshape(8, 16, 128)
        for i in range(3):
            lanes = slice(i * C + at, i * C + at + 128)
            grad_packed[:, half, :, lanes] = results[i][n].reshape(8, 16, 128)

    mixed_out[...] = blended[...].reshape(256, C)
    weight_gradient(1 - pos[3], normal, mixed_out, tile, grad_packed, send)


def gradient_pair(first, second):
    def gap(n):
        return jnp.zeros((256, n), BF16)

    def placed(left, *parts):
        return mm_tn(left, jnp.concatenate(parts, axis=1))

    a = placed(first[0], first[2], gap(16))
    b = placed(first[1], gap(112), first[3], gap(64))
    c = placed(second[0], gap(64), second[2], gap(80))
    d = placed(second[1], gap(48), second[3])
    groups = (
        a[:, :128],
        a[:, 128:] + b[:, :128],
        b[:, 128:] + c[:, :128],
        c[:, 128:256],
        c[:, 256:] + d,
    )
    return jnp.concatenate(groups, axis=1).astype(BF16)


def weight_gradient(core, normal, mixed, tile, grad_packed, target):
    for which in range(2):

        @pl.when(core == which)
        def _(which=which):
            packed = grad_packed[...].reshape(256, 3 * C)
            arriving = tile[:, 1].reshape(256, C)
            left, right = normal[...], mixed[...]

            def sides(x):
                at = 2 * x + which
                return packed[:, 240 * at : 240 * at + 240], arriving[:, 80 * at : 80 * at + 80]

            if which == 0:
                for half in range(2):
                    a, b = [(left, right) + sides(2 * half + i) for i in range(2)]
                    both = gradient_pair(a, b).reshape(2, 4, 80, C)
                    for zl in range(2):
                        target[:, 2 * zl + half] = both[zl]
            else:
                lefts = left[:, :320], left[:, 320:]
                rights = right[:, :320], right[:, 320:]
                for x in range(4):
                    a, b = [(lefts[zl], rights[zl]) + sides(x) for zl in range(2)]
                    target[x] = gradient_pair(a, b).reshape(4, 80, C)


def own_gradient_body(pos, normal, mixed, tile, grad_packed, keep):
    weight_gradient(pos[3], normal, mixed, tile, grad_packed, keep)


def own_gradient(normal, mixed, tile, grad_packed):
    return call(
        own_gradient_body,
        [sds(BLOCKS)],
        4,
        0,
        limit=24,
        flops=2 * 256 * 2 * C * C,
        moved=2 * C * C * 2,
    )(normal, mixed, tile, grad_packed)[0]


def attention_step(normal, tile, weight):
    return call(
        attention_body,
        [sds((8, 2, 16, 3 * C)), sds((256, C)), sds(BLOCKS)],
        3,
        0,
        (
            pltpu.VMEM((8, 2, 16, 3 * C), BF16),
            pltpu.VMEM((8, 2, 16, C), BF16),
            pltpu.VMEM((8, 2, 16, C), BF16),
        ),
        limit=32,
        flops=2 * 256 * 8 * C * C,
        moved=4 * C * C * 2,
    )(normal, tile, weight)


def tile_gradient_body(pos, *refs):
    grad_packed, temporal, tile, gain, weight_ref, time_ref, _, out, padded = refs
    weight = weight_ref[...].reshape(C, 4 * C)[:, : 3 * C]
    grad_normal = mm_nt(grad_packed[...].reshape(256, 3 * C), weight)
    value = temporal[...].astype(F32)
    scale = lax.rsqrt(jnp.mean(value * value, axis=-1, keepdims=True) + 1e-06)
    scaled = grad_normal * gain[...]
    inner = jnp.mean(value * scaled, axis=-1, keepdims=True)
    through_norm = scale * scaled - value * (scale * scale * scale * inner)
    grad_temporal = (tile[:, 1].astype(F32).reshape(256, C) + through_norm).astype(BF16)
    padded[0] = jnp.zeros((32, C), BF16)
    padded[1:9] = grad_temporal.reshape(8, 32, C)
    padded[9] = jnp.zeros((32, C), BF16)
    taps = time_ref[...].reshape(3 * C, C)
    grad_act = jnp.zeros((256, C), F32)
    for k in range(3):
        later = padded[2 - k : 10 - k].reshape(256, C)
        grad_act = grad_act + mm_nt(later, taps[k * C : (k + 1) * C, :])
    as_float = tile[:, 0].astype(F32).reshape(256, C)
    logistic = jax.nn.sigmoid(as_float)
    grad_spatial = grad_temporal.astype(F32) + grad_act * logistic * (
        1.0 + as_float * (1.0 - logistic)
    )
    out[...] = grad_spatial.astype(BF16).reshape(8, 32, C)


def tile_gradient(grad_packed, temporal, tile, gain, weight, time, after):
    return call(
        tile_gradient_body,
        [sds((8, 32, C))],
        6,
        1,
        PADDED,
        limit=24,
        flops=2 * 256 * 6 * C * C,
        moved=7 * C * C * 2,
    )(grad_packed, temporal, tile, gain, weight, time, after)[0]


def pair_sum_body(pos, keep, other, own, *sends):
    me = jnp.where(pos[3] == 0, pos[1], pos[2])

    def block(index):
        return keep[index].astype(F32) + other[index].astype(F32)

    own[...] = block(me)
    for k in range(3):
        sends[k][...] = block((me + k + 1) % 4).astype(BF16)


def second_sum_body(pos, held, *refs):
    others, own, sends, scratch = refs[0:3], refs[3], refs[4:7], refs[7]
    total = held[...]
    for other in others:
        total = total + other[...].astype(F32)

    for which in range(2):

        @pl.when(pos[3] == which)
        def _(which=which):
            for i in range(4):
                for zl in range(2):
                    block, at = (2 * zl + i // 2, i % 2) if which == 0 else (i, zl)
                    scratch[i, zl] = total[block, :, 320 * at : 320 * at + 320]

    me = jnp.where(pos[3] == 0, pos[2], pos[1])
    own[...] = scratch[me]
    for k in range(3):
        sends[k][...] = scratch[(me + k + 1) % 4].astype(BF16)


def third_sum_body(pos, held, first, second, third, out):
    total = held[...]
    for other in (first, second, third):
        total = total + other[...].astype(F32)
    for row in range(4):
        out[row, :, :, 0:60] = total[:, :, 60 * row : 60 * row + 60].astype(BF16)
        out[row, :, :, 60:80] = total[:, :, 240 + 20 * row : 240 + 20 * row + 20].astype(BF16)


def row_sum_body(pos, parts, after, own, send, scratch):
    scratch[...] = jnp.sum(parts[...].astype(F32), axis=0)
    own[...] = scratch[pos[0]]
    send[...] = scratch[1 - pos[0]].astype(BF16)


def last_sum_body(pos, held, other, qkv_out, out_out):
    total = (held[...] + other[...].astype(F32)).T
    qkv_out[...] = total[0:60]
    out_out[...] = total[60:80]


def round_trip(sends, axis):
    return [
        lax.ppermute(sends[k], axis, [(i, (i + k + 1) % 4) for i in range(4)]) for k in range(3)
    ]


def crosswise(sends, first):
    def target(y, x, core, k):
        if (core == 0) == first:
            return (y + k + 1) % 4, x
        return y, (x + k + 1) % 4

    moved = []
    for k in range(3):
        pairs = []
        for y in range(4):
            for x in range(4):
                for core in range(2):
                    ty, tx = target(y, x, core, k)
                    pairs.append(((y * 4 + x) * 2 + core, (ty * 4 + tx) * 2 + core))
        moved.append(lax.ppermute(sends[k], ("y", "x", "c"), pairs))
    return moved


def pair_sum(keep, send):
    step = BLOCKS[1:]
    return call(pair_sum_body, [sds(step, F32)] + [sds(step)] * 3, 2, 0, limit=20)(
        keep, swapped(send)
    )


def reduce_grads(summed, after):
    own, *sends = summed
    step = (2, 80, 320)
    own, *sends = call(
        second_sum_body,
        [sds(step, F32)] + [sds(step)] * 3,
        4,
        0,
        (pltpu.VMEM((4,) + step, F32),),
        limit=20,
    )(own, *crosswise(sends, True))
    parts = call(third_sum_body, [sds((4, 2, 80, 80))], 4, 0)(own, *crosswise(sends, False))[0]
    parts = lax.all_to_all(parts, "zh", split_axis=0, concat_axis=0, tiled=True)
    own, send = call(
        row_sum_body, [sds((80, 80), F32), sds((80, 80))], 1, 1, (pltpu.VMEM((2, 80, 80), F32),)
    )(parts, after)
    other = lax.ppermute(send, "zl", [(0, 1), (1, 0)])
    grads = call(last_sum_body, [sds((60, 80), F32), sds((20, 80), F32)], 2, 0)(own, other)
    return [grad.T for grad in grads]


def edges(top, bottom):
    low = lax.ppermute(bottom, "zh", [(i, (i + 1) % 4) for i in range(4)])
    high = lax.ppermute(top, "zh", [(i, (i + 3) % 4) for i in range(4)])
    return low, high


def exchange(rows):
    return lax.all_to_all(rows, FRAME, split_axis=0, concat_axis=0, tiled=True)


def shards(latents, space_kernel, time_kernel, qkv_weight, out_weight, norm_gain, grad_out):
    images, incoming = latents[0, 0], grad_out[0, 0]
    gain = norm_gain.reshape(1, C)
    half, twin, top, bottom = halves_of(time_kernel, qkv_weight, out_weight, images)
    others = round_trip([half] * 3, "y")
    low, high = edges(top, bottom)
    near = across(gate(twin, high))
    rows = conv_forward(images, low, high, incoming, space_kernel)
    tile = exchange(rows)
    own, three = four_of(half, others, rows, near)
    far = gate(across(three), tile)
    weights = [own, swapped(own), near, swapped(near), far, swapped(far)]
    temporal, normal, time, weight = temporal_step(tile, gain, weights)
    grad_packed, mixed, send = attention_step(normal, tile, weight)
    keep = own_gradient(normal, mixed, tile, grad_packed)
    summed = pair_sum(keep, send)
    grad_spatial = exchange(
        tile_gradient(grad_packed, temporal, tile, gain, weight, time, summed[0])
    )
    low, high = edges(grad_spatial[0:1], grad_spatial[7:8])
    grad_latents, token = conv_backward(grad_spatial, low, high, space_kernel)
    grad_qkv, grad_outproj = reduce_grads(summed, token)
    return grad_latents[None, None], grad_qkv, grad_outproj


def solution(mesh):
    inner = Mesh(mesh.devices.reshape(2, 4, 4, 2, 4), ("zl", "y", "x", "c", "zh"))
    tiles = P(VIDEO, FRAME, "zh", None, None)
    weight = P(VIDEO, None)
    grads = P(VIDEO, ("x", "c", "zh"))
    return jax.shard_map(
        shards,
        mesh=inner,
        in_specs=(tiles, P(), weight, weight, weight, P(), tiles),
        out_specs=(tiles, grads, grads),
        check_vma=False,
    )
```
